128 devices in a mesh: section: 2 (over x_hi), view: 16 (over x_lo, y, core), dp: 4 (over z).
Axes of the slice: x: 4 (x_hi: 2, x_lo: 2; x = x_hi * 2 + x_lo), y: 4, z: 4, core: 2. Of those that a mesh axis runs over, the one named last changes fastest.
Arguments:
- scenes: bfloat16 [8, 16, 128, 1024], P('dp', 'view'), may hold values from -6 to 6
- neighbours: int32 [8, 16, 3], P('dp', 'view'), may hold values from 0 to 15, as said below
- counts: int32 [8, 16], P('dp', 'view'), may hold values from 1 to 3, as said below
- w_in: bfloat16 [2, 1024, 3072], P('section'), may hold values from -8 to 8
- w_out: bfloat16 [2, 1024, 1024], P('section'), may hold values from -1.5 to 1.5
- cotangent: bfloat16 [8, 16, 128, 1024], P('dp', 'view'), may hold values from -3 to 3
Outputs:
- section_outputs: bfloat16 [2, 8, 16, 128, 1024], P('section', 'dp', 'view')
- input_grads: bfloat16 [2, 8, 16, 128, 1024], P('section', 'dp', 'view')
- grad_w_in: float32 [2, 1024, 3072], P('section', ('view', 'dp'))
- grad_w_out: float32 [2, 1024, 1024], P('section', ('view', 'dp'))
The draws below stay inside these ranges and needn't reach their ends.
Inputs may be any that keep to these rules, and one draw needn't show every extreme that they name: In slots below the view's count, neighbours names distinct views at cycle distance 1 to 2 from the view (index difference modulo 16); the other slots name the view itself. `counts`: in every scene some view has 3 live slots.
All inputs are finite; a program needn't handle non-finite values.
Results may differ from the reference program's by a relative error of at most 0.028.
Values may be sent and summed in bfloat16 or wider, within the bound.
A program may use at most 128 MiB of HBM per device.

```python
import math
import jax
import jax.numpy as jnp
from jax import lax

D = 1024
HEADS = 8
HEAD_DIM = 128
TOK = 128
SECTIONS = 2
VIEWS = 16
SCENES = 8
SPAN = 2
NBR = 3


def pick_graph(key):
    ranking = jax.random.randint(jax.random.fold_in(key, 11), (SCENES, VIEWS, 2 * SPAN), 0, 1 << 20)
    ranking = ranking * (2 * SPAN) + jnp.arange(2 * SPAN, dtype=jnp.int32)
    ordering = jnp.argsort(ranking, axis=-1, stable=True)
    table = jnp.concatenate([jnp.arange(-SPAN, 0, dtype=jnp.int32), jnp.arange(1, SPAN + 1, dtype=jnp.int32)])
    chosen = table[ordering[..., :NBR]]
    view_count = jax.random.randint(jax.random.fold_in(key, 12), (SCENES, VIEWS), 1, NBR + 1)
    full_view = jax.random.randint(jax.random.fold_in(key, 13), (SCENES, 1), 0, VIEWS)
    view_ids = jnp.arange(VIEWS, dtype=jnp.int32)
    view_count = jnp.where(view_ids[None, :] == full_view, NBR, view_count)
    slot_ids = jnp.arange(NBR, dtype=jnp.int32)
    listed = jnp.where(slot_ids[None, None, :] < view_count[..., None], (view_ids[None, :, None] + chosen) % VIEWS, view_ids[None, :, None])
    return (listed.astype(jnp.int32), view_count.astype(jnp.int32))


def draw_neighbours(key, part):
    graph = pick_graph(key)
    return graph[0]


def draw_counts(key, part):
    graph = pick_graph(key)
    return graph[1]


def draw_scenes(key, part):
    key = jax.random.fold_in(key, 3)
    shape = (SCENES, VIEWS, TOK, D)
    sample = jax.random.normal(jax.random.fold_in(key, 1), shape, jnp.float32)
    return jnp.clip(sample, -6.0, 6.0).astype(jnp.bfloat16)


def draw_w_in(key, part):
    key = jax.random.fold_in(key, 5)
    shape = (SECTIONS, D, 3 * D)
    sample = jax.random.normal(jax.random.fold_in(key, 1), shape, jnp.float32) / math.sqrt(D)
    return jnp.clip(sample, -8.0, 8.0).astype(jnp.bfloat16)


def level_of(key, dims, shards, low, top_value):
    def one(axis_at, blocks):
        draws = jax.random.uniform(jax.random.fold_in(jax.random.fold_in(key, 6), axis_at), (blocks,), jnp.float32, low / len(shards), top_value / len(shards))
        return jnp.repeat(jnp.exp(draws), dims[axis_at] // blocks).reshape((-1,) + (1,) * (len(dims) - axis_at - 1))

    factor_of = one(*shards[0])
    for cut in shards[1:]:
        factor_of = factor_of * one(*cut)
    return factor_of


def bell_draw(own_key, extent, width, most, pieces=(), kind=jnp.bfloat16):
    result = width * jax.random.normal(own_key, extent, jnp.float32)
    if pieces:
        result = result * level_of(own_key, extent, pieces, -0.22, 0.18)
    return jnp.clip(result, -most, most).astype(kind)


def setup_inputs(seed: int = 0) -> dict:
    key_list = jax.random.split(jax.random.key(seed), 7)
    return {
        "scenes": draw_scenes(jax.random.fold_in(key_list[6], 71), 0),
        "neighbours": draw_neighbours(jax.random.fold_in(key_list[6], 71), 0),
        "counts": draw_counts(jax.random.fold_in(key_list[6], 71), 0),
        "w_in": draw_w_in(jax.random.fold_in(key_list[6], 71), 0),
        "w_out": bell_draw(key_list[4], (SECTIONS, D, D), (D // 64) ** -0.5, 1.5, ((0, 2),)),
        "cotangent": bell_draw(key_list[5], (SCENES, VIEWS, TOK, D), 0.5, 3.0, ((0, 4), (1, 16))),
    }


EPSILON = 1e-06
NEGATIVE = -1e+30

def section_forward(section_input, weight_in, weight_out, neighbour_ids, view_counts):
    upcast = section_input.astype(jnp.float32)
    factor = lax.rsqrt(lax.optimization_barrier(jnp.mean(upcast * upcast, -1, keepdims=True)) + EPSILON)
    normed = (upcast * factor).astype(jnp.bfloat16)
    projected = jnp.dot(normed.reshape(VIEWS * TOK, D), weight_in, preferred_element_type=jnp.float32)
    projected = projected.astype(jnp.bfloat16).reshape(VIEWS, TOK, 3 * D)
    queries = projected[:, :, :D]
    keyval = projected[:, :, D:]
    blocks = jnp.concatenate([keyval[:, None], keyval[neighbour_ids]], 1)
    slot_live = jnp.arange(NBR, dtype=jnp.int32)[None, :] < view_counts[:, None]
    block_live = jnp.concatenate([jnp.ones((VIEWS, 1), dtype=bool), slot_live], 1)
    key_live = jnp.repeat(block_live, TOK, axis=1)
    key_rows = blocks[..., :D].reshape(VIEWS, (NBR + 1) * TOK, HEADS, HEAD_DIM)
    value_rows = blocks[..., D:].reshape(VIEWS, (NBR + 1) * TOK, HEADS, HEAD_DIM)
    query_heads = queries.reshape(VIEWS, TOK, HEADS, HEAD_DIM)
    key_scale = 1.0 / math.sqrt(HEAD_DIM)
    scores = jnp.einsum('vnhe,vkhe->vhnk', query_heads.astype(jnp.float32), key_rows.astype(jnp.float32)) * key_scale
    live_mask = key_live[:, None, None, :]
    masked = jnp.where(live_mask, scores, NEGATIVE)
    row_max = lax.optimization_barrier(jnp.max(masked, -1, keepdims=True))
    exp_terms = jnp.where(live_mask, jnp.exp(masked - row_max), 0.0)
    attn_prob = exp_terms / lax.optimization_barrier(jnp.sum(exp_terms, -1, keepdims=True))
    prob_low = attn_prob.astype(jnp.bfloat16)
    attended = jnp.einsum('vhnk,vkhe->vnhe', prob_low.astype(jnp.float32), value_rows.astype(jnp.float32))
    attended = attended.astype(jnp.bfloat16).reshape(VIEWS, TOK, D)
    branch = jnp.dot(attended.reshape(VIEWS * TOK, D), weight_out, preferred_element_type=jnp.float32)
    section_output = (upcast + branch.reshape(VIEWS, TOK, D)).astype(jnp.bfloat16)
    kept = (section_input, factor, normed, queries, blocks, attn_prob, attended)
    return (section_output, kept)

def section_backward(kept, out_grad, weight_in, weight_out, neighbour_ids):
    section_input, factor, normed, queries, blocks, attn_prob, attended = kept
    key_scale = 1.0 / math.sqrt(HEAD_DIM)
    attn_grad = jnp.dot(out_grad.reshape(VIEWS * TOK, D), weight_out.T, preferred_element_type=jnp.float32)
    attn_grad = attn_grad.astype(jnp.bfloat16).reshape(VIEWS, TOK, HEADS, HEAD_DIM)
    key_rows = blocks[..., :D].reshape(VIEWS, (NBR + 1) * TOK, HEADS, HEAD_DIM)
    value_rows = blocks[..., D:].reshape(VIEWS, (NBR + 1) * TOK, HEADS, HEAD_DIM)
    query_heads = queries.reshape(VIEWS, TOK, HEADS, HEAD_DIM)
    prob_grad = jnp.einsum('vnhe,vkhe->vhnk', attn_grad.astype(jnp.float32), value_rows.astype(jnp.float32))
    row_dot = lax.optimization_barrier(jnp.sum(attn_prob * prob_grad, -1, keepdims=True))
    score_grad = (attn_prob * (prob_grad - row_dot) * key_scale).astype(jnp.bfloat16)
    query_grad = jnp.einsum('vhnk,vkhe->vnhe', score_grad.astype(jnp.float32), key_rows.astype(jnp.float32))
    query_grad = query_grad.astype(jnp.bfloat16).reshape(VIEWS, TOK, D)
    key_part = jnp.einsum('vhnk,vnhe->vkhe', score_grad.astype(jnp.float32), query_heads.astype(jnp.float32))
    prob_low = attn_prob.astype(jnp.bfloat16)
    value_part = jnp.einsum('vhnk,vnhe->vkhe', prob_low.astype(jnp.float32), attn_grad.astype(jnp.float32))
    keyval_part = jnp.concatenate([key_part.reshape(VIEWS, NBR + 1, TOK, D), value_part.reshape(VIEWS, NBR + 1, TOK, D)], -1)
    sent = lax.optimization_barrier(keyval_part[:, 1:].astype(jnp.bfloat16)).astype(jnp.float32)
    summed = keyval_part[:, 0].at[neighbour_ids].add(sent)
    proj_grad = jnp.concatenate([query_grad, summed.astype(jnp.bfloat16)], -1)
    normed_grad = jnp.dot(proj_grad.reshape(VIEWS * TOK, 3 * D), weight_in.T, preferred_element_type=jnp.float32)
    normed_grad = normed_grad.reshape(VIEWS, TOK, D)
    unit_rows = section_input.astype(jnp.float32) * factor
    inner = lax.optimization_barrier(jnp.mean(normed_grad * unit_rows, -1, keepdims=True))
    input_grad = (out_grad.astype(jnp.float32) + factor * (normed_grad - unit_rows * inner)).astype(jnp.bfloat16)
    part_in = jnp.dot(normed.reshape(VIEWS * TOK, D).T, proj_grad.reshape(VIEWS * TOK, 3 * D), preferred_element_type=jnp.float32)
    part_out = jnp.dot(attended.reshape(VIEWS * TOK, D).T, out_grad.reshape(VIEWS * TOK, D), preferred_element_type=jnp.float32)
    return (input_grad, part_in, part_out)

def reference(scenes, neighbours, counts, w_in, w_out, cotangent):

    def one_scene(carry, packed):
        scene_rows, neighbour_ids, view_counts, scene_cot = packed
        output_list = []
        kept_list = []
        current = scene_rows
        for section_no in range(SECTIONS):
            current, kept = section_forward(current, w_in[section_no], w_out[section_no], neighbour_ids, view_counts)
            output_list.append(current)
            kept_list.append(kept)
        grad_list = [current] * SECTIONS
        sums_in = [carry[0][0]] * SECTIONS
        sums_out = [carry[1][0]] * SECTIONS
        flowing = scene_cot
        for section_no in reversed(range(SECTIONS)):
            flowing, part_in, part_out = section_backward(kept_list[section_no], flowing, w_in[section_no], w_out[section_no], neighbour_ids)
            grad_list[section_no] = flowing
            sums_in[section_no] = carry[0][section_no] + part_in
            sums_out[section_no] = carry[1][section_no] + part_out
        return ((jnp.stack(sums_in), jnp.stack(sums_out)), (jnp.stack(output_list), jnp.stack(grad_list)))
    start = (jnp.zeros((SECTIONS, D, 3 * D), jnp.float32), jnp.zeros((SECTIONS, D, D), jnp.float32))
    totals, stacked = lax.scan(one_scene, start, (scenes, neighbours, counts, cotangent))
    section_outputs = jnp.swapaxes(stacked[0], 0, 1)
    input_grads = jnp.swapaxes(stacked[1], 0, 1)
    return (section_outputs, input_grads, totals[0] / SCENES, totals[1] / SCENES)
```

```python
import functools
import math

import jax
import jax.numpy as jnp
from jax import lax
from jax.experimental import pallas as pl
from jax.experimental.pallas import tpu as pltpu
from jax.sharding import PartitionSpec as P

MESH = pl.DeviceIdType.MESH

HEADS = 8
HEAD_DIM = 128


EPSILON = 1e-06
NEGATIVE = -1e30


CHUNK = 512
PAIRS = ((6, 7), (0, 1), (2, 3), (4, 5))


def wgrad_kernel(
    share, nT, aT, proj, og, gin, gout,
    nT_r, aT_r, proj_r, og_r, G, r1, r2, r3, r4, r5,
    xs, xr, ss, rs,
):
    view = lax.axis_index("view")
    zi = lax.axis_index("dp")
    core = lax.rem(view, 2)
    yi = lax.rem(view // 2, 4)
    xi = view // 8
    peer = xi * 8 + yi * 2 + (1 - core)
    across = (1 - xi) * 8 + yi * 2 + core

    def y_dev(step):
        return {"view": xi * 8 + lax.rem(yi + step + 4, 4) * 2 + core}

    def z_dev(step):
        return {"dp": lax.rem(zi + step + 4, 4)}

    barrier = pltpu.get_barrier_semaphore()
    partners = ({"view": peer}, {"view": across}, y_dev(1), y_dev(-1), z_dev(1), z_dev(-1))
    for dev in partners:
        pl.semaphore_signal(barrier, inc=1, device_id=dev, device_id_type=MESH)
    pl.semaphore_wait(barrier, len(partners))

    def remote(src, dst, s, r, dev):
        return pltpu.make_async_remote_copy(
            src_ref=src, dst_ref=dst, send_sem=s, recv_sem=r, device_id=dev, device_id_type=MESH
        )

    def cols(ref, k):
        return ref.at[:, pl.ds(k * CHUNK, CHUNK)]

    pieces = {}
    pieces["a"] = remote(aT.at[:, 1 - core], aT_r, xs.at[8], xr.at[8], {"view": peer})
    pieces["n"] = remote(nT.at[:, 1 - core], nT_r, xs.at[9], xr.at[9], {"view": peer})
    for n in range(6):
        pieces[n] = remote(cols(proj, n), cols(proj_r, n), xs.at[n], xr.at[n], {"view": peer})
    for n in range(6, 8):
        pieces[n] = remote(
            cols(og, n - 6), cols(og_r, n - 6), xs.at[n], xr.at[n], {"view": peer}
        )
    for key in ("a", 6, 7, "n", 0, 1, 2, 3, 4, 5):
        pieces[key].start()

    def first(n, x_at, a):
        return G.at[n, x_at, a] if n % 2 == 0 else G.at[n, x_at, :, a]

    def second(n, x_at, a, b):
        return G.at[n, x_at, a, b] if n % 2 == 0 else G.at[n, x_at, b, a]

    whole = slice(None)
    sent = []

    def send(n, k, src, dst, dev):
        copy = remote(src, dst, ss.at[n, k], rs.at[n, k], dev)
        copy.start()
        sent.append(copy)
        return copy

    arrived = {}

    def add_into(ref, *others):
        total = ref[...].astype(jnp.float32)
        for other in others:
            total = total + other[...].astype(jnp.float32)
        ref[...] = total.astype(jnp.bfloat16)

    seen = set()

    def need(key):
        if key not in seen:
            seen.add(key)
            pieces[key].wait_recv()

    def stage(n, s):
        a, b = (yi, zi) if n % 2 == 0 else (zi, yi)
        dev1, dev2 = (y_dev, z_dev) if n % 2 == 0 else (z_dev, y_dev)
        if s == 0:
            if n >= 6:
                need("a")
                left, left_r, right, right_r, k = aT, aT_r, og, og_r, n - 6
            else:
                need("n")
                left, left_r, right, right_r, k = nT, nT_r, proj, proj_r, n
            need(n)
            rows = left.shape[0] * left.shape[2]
            toks = left.shape[3]
            mine = left[:, core].reshape(rows, toks)
            theirs = left_r[...].reshape(rows, toks)
            part = jnp.dot(
                mine, right[:, k * CHUNK : (k + 1) * CHUNK], preferred_element_type=jnp.float32
            ) + jnp.dot(
                theirs, right_r[:, k * CHUNK : (k + 1) * CHUNK], preferred_element_type=jnp.float32
            )
            G[n] = part.astype(jnp.bfloat16).reshape(G.shape[1:])
            opp = lax.rem(a + 2, 4)
            arrived[n, 0] = (
                send(n, 0, first(n, 0, opp), r1.at[n, 0], dev1(1)),
                send(n, 1, first(n, 1, opp), r1.at[n, 1], dev1(-1)),
            )
            return
        for copy in arrived[n, s - 1]:
            copy.wait_recv()
        if s == 1:
            up, down = lax.rem(a + 1, 4), lax.rem(a + 3, 4)
            add_into(first(n, 0, up), r1.at[n, 0])
            add_into(first(n, 1, down), r1.at[n, 1])
            arrived[n, 1] = (
                send(n, 2, first(n, whole, up), r2.at[n, 0], dev1(1)),
                send(n, 3, first(n, whole, down), r2.at[n, 1], dev1(-1)),
            )
        elif s == 2:
            add_into(first(n, whole, a), r2.at[n, 0], r2.at[n, 1])
            opp = lax.rem(b + 2, 4)
            arrived[n, 2] = (
                send(n, 4, second(n, 0, a, opp), r3.at[n, 0], dev2(1)),
                send(n, 5, second(n, 1, a, opp), r3.at[n, 1], dev2(-1)),
            )
        elif s == 3:
            up, down = lax.rem(b + 1, 4), lax.rem(b + 3, 4)
            add_into(second(n, 0, a, up), r3.at[n, 0])
            add_into(second(n, 1, a, down), r3.at[n, 1])
            arrived[n, 3] = (
                send(n, 6, second(n, whole, a, up), r4.at[n, 0], dev2(1)),
                send(n, 7, second(n, whole, a, down), r4.at[n, 1], dev2(-1)),
            )
        elif s == 4:
            add_into(second(n, whole, a, b), r4.at[n, 0], r4.at[n, 1])
            arrived[n, 4] = (
                send(n, 8, second(n, 1 - xi, a, b), r5.at[n], {"view": across}),
            )
        else:
            total = second(n, xi, a, b)[...].astype(jnp.float32) + r5[n].astype(jnp.float32)
            out, k = (gin, n) if n < 6 else (gout, n - 6)
            out[:, k * CHUNK : (k + 1) * CHUNK] = total * share

    stages = 6
    for turn in range(len(PAIRS) + stages - 1):
        for p in range(len(PAIRS)):
            s = turn - p
            if 0 <= s < stages:
                for n in PAIRS[p]:
                    stage(n, s)
    for copy in list(pieces.values()) + sent:
        copy.wait_send()


def weight_grads(normed, attended, proj, outgrad, share):
    toks, width = normed.shape
    chunks = 4 * width // CHUNK
    nT = normed.T.reshape(8, 2, width // 16, toks)
    aT = attended.T.reshape(8, 2, width // 16, toks)
    rows = width // 64
    vm = pl.BlockSpec(memory_space=pltpu.VMEM)
    bf = jnp.bfloat16
    return pl.pallas_call(
        functools.partial(wgrad_kernel, share),
        out_shape=(
            jax.ShapeDtypeStruct((rows, 3 * width), jnp.float32),
            jax.ShapeDtypeStruct((rows, width), jnp.float32),
        ),
        in_specs=[vm] * 4,
        out_specs=(vm, vm),
        scratch_shapes=[
            pltpu.VMEM((8, width // 16, toks), bf),
            pltpu.VMEM((8, width // 16, toks), bf),
            pltpu.VMEM((toks, 3 * width), bf),
            pltpu.VMEM((toks, width), bf),
            pltpu.VMEM((chunks, 2, 4, 4, rows, CHUNK), bf),
            pltpu.VMEM((chunks, 2, 4, rows, CHUNK), bf),
            pltpu.VMEM((chunks, 2, 2, 4, rows, CHUNK), bf),
            pltpu.VMEM((chunks, 2, rows, CHUNK), bf),
            pltpu.VMEM((chunks, 2, 2, rows, CHUNK), bf),
            pltpu.VMEM((chunks, rows, CHUNK), bf),
            pltpu.SemaphoreType.DMA((10,)),
            pltpu.SemaphoreType.DMA((10,)),
            pltpu.SemaphoreType.DMA((chunks, 9)),
            pltpu.SemaphoreType.DMA((chunks, 9)),
        ],
        compiler_params=pltpu.CompilerParams(
            collective_id=1, has_side_effects=True, vmem_limit_bytes=40 * 1024 * 1024
        ),
        cost_estimate=pl.CostEstimate(
            flops=2 * 512 * 512 * 4096, bytes_accessed=4 << 20, transcendentals=0
        ),
    )(nT, aT, proj, outgrad)


def from_behind(value, axis, steps):
    count = lax.axis_size(axis)
    pairs = [(source, (source + steps) % count) for source in range(count)]
    return lax.ppermute(value, axis, pairs)


def from_behind_2(block, axis, distance):
    devices = range(lax.axis_size(axis))
    route = [(i - distance, i) for i in devices if i - distance in devices]
    return lax.ppermute(block, axis, route)


def attend_rows(queries, blocks, block_live, token_rows, model_width):
    block_total = blocks.shape[0]
    key_rows = blocks[..., :model_width].reshape(block_total * token_rows, HEADS, HEAD_DIM)
    value_rows = blocks[..., model_width:].reshape(block_total * token_rows, HEADS, HEAD_DIM)
    query_heads = queries.reshape(token_rows, HEADS, HEAD_DIM)
    key_scale = 1.0 / math.sqrt(HEAD_DIM)
    scores = (
        jnp.einsum("nhe,khe->hnk", query_heads, key_rows, preferred_element_type=jnp.float32)
        * key_scale
    )
    key_live = jnp.repeat(block_live, token_rows)[None, None, :]
    masked = jnp.where(key_live, scores, NEGATIVE)
    row_max = jnp.max(masked, -1, keepdims=True)
    exp_terms = jnp.where(key_live, jnp.exp(masked - row_max), 0.0)
    attn_prob = exp_terms / jnp.sum(exp_terms, -1, keepdims=True)
    prob_low = attn_prob.astype(jnp.bfloat16)
    attended = jnp.einsum("hnk,khe->nhe", prob_low, value_rows, preferred_element_type=jnp.float32)
    return (attn_prob, attended.reshape(token_rows, model_width).astype(jnp.bfloat16))


def take_tick(stacked, position):
    return lax.dynamic_index_in_dim(stacked, position, 0, keepdims=False)


def on_device(scenes, neighbours, counts, w_in, w_out, cotangent):
    view_total = lax.axis_size("view")
    section_total = lax.axis_size("section")
    reach = min(2, (view_total - 1) // 2)
    offsets = list(range(-reach, 0)) + list(range(1, reach + 1))
    micro_total = scenes.shape[0]
    token_rows = scenes.shape[2]
    model_width = scenes.shape[3]
    slot_total = neighbours.shape[2]
    tick_total = micro_total + section_total - 1
    section_no = lax.axis_index("section")
    view_no = lax.axis_index("view")
    weight_in = w_in[0]
    weight_out = w_out[0]
    key_scale = 1.0 / math.sqrt(HEAD_DIM)
    view_rel = (neighbours[:, 0, :] - view_no) % view_total
    signed_rel = jnp.where(view_rel <= reach, view_rel, view_rel - view_total)
    slot_place = jnp.where(signed_rel < 0, signed_rel + reach, signed_rel + reach - 1)
    slot_live = jnp.arange(slot_total, dtype=jnp.int32)[None, :] < counts
    slot_pick = (slot_place[..., None] == jnp.arange(2 * reach, dtype=jnp.int32)) & slot_live[
        ..., None
    ]
    incoming = jnp.zeros((token_rows, model_width), jnp.bfloat16)
    input_list, factor_list, normed_list, query_list = ([], [], [], [])
    block_list, live_list, prob_list, attended_list, output_list = ([], [], [], [], [])
    for tick_no in range(tick_total):
        micro_index = jnp.clip(tick_no - section_no, 0, micro_total - 1)
        first_rows = scenes[min(tick_no, micro_total - 1), 0]
        section_input = jnp.where(section_no == 0, first_rows, incoming)
        upcast = section_input.astype(jnp.float32)
        factor = lax.rsqrt(jnp.mean(upcast * upcast, -1, keepdims=True) + EPSILON)
        normed = (upcast * factor).astype(jnp.bfloat16)
        projected = jnp.dot(normed, weight_in, preferred_element_type=jnp.float32).astype(
            jnp.bfloat16
        )
        queries = projected[:, :model_width]
        keyval = projected[:, model_width:]
        fetched = []
        for offset in offsets:
            fetched.append(from_behind(keyval, "view", -offset))
        candidates = jnp.stack(fetched)
        place_now = take_tick(slot_place, micro_index)
        live_now = take_tick(slot_live, micro_index)
        remote = jnp.take(candidates, place_now, axis=0)
        blocks = jnp.concatenate([keyval[None], remote], 0)
        block_live = jnp.concatenate([jnp.ones((1,), dtype=bool), live_now], 0)
        attn_prob, attended = attend_rows(queries, blocks, block_live, token_rows, model_width)
        branch = jnp.dot(attended, weight_out, preferred_element_type=jnp.float32)
        section_output = (upcast + branch).astype(jnp.bfloat16)
        incoming = from_behind_2(section_output, "section", 1)
        input_list.append(section_input)
        factor_list.append(factor)
        normed_list.append(normed)
        query_list.append(queries)
        block_list.append(blocks)
        live_list.append(block_live)
        prob_list.append(attn_prob)
        attended_list.append(attended)
        output_list.append(section_output)
    input_stack = jnp.stack(input_list)
    factor_stack = jnp.stack(factor_list)
    query_stack = jnp.stack(query_list)
    block_stack = jnp.stack(block_list)
    prob_stack = jnp.stack(prob_list)
    incoming_grad = jnp.zeros((token_rows, model_width), jnp.bfloat16)
    grad_list, proj_list, outgrad_list = ([], [], [])
    for tick_no in range(tick_total):
        micro_index = jnp.clip(tick_no - (section_total - 1 - section_no), 0, micro_total - 1)
        saved_tick = jnp.clip(tick_no - section_total + 1 + 2 * section_no, 0, tick_total - 1)
        section_input = take_tick(input_stack, saved_tick)
        factor = take_tick(factor_stack, saved_tick)
        queries = take_tick(query_stack, saved_tick)
        blocks = take_tick(block_stack, saved_tick)
        attn_prob = take_tick(prob_stack, saved_tick)
        block_total = blocks.shape[0]
        last_rows = take_tick(cotangent[:, 0], micro_index)
        out_grad = jnp.where(section_no == section_total - 1, last_rows, incoming_grad)
        attn_grad = jnp.einsum(
            "nf,df->nd", out_grad, weight_out, preferred_element_type=jnp.float32
        ).astype(jnp.bfloat16)
        grad_heads = attn_grad.reshape(token_rows, HEADS, HEAD_DIM)
        key_rows = blocks[..., :model_width].reshape(block_total * token_rows, HEADS, HEAD_DIM)
        value_rows = blocks[..., model_width:].reshape(block_total * token_rows, HEADS, HEAD_DIM)
        query_heads = queries.reshape(token_rows, HEADS, HEAD_DIM)
        prob_grad = jnp.einsum(
            "nhe,khe->hnk", grad_heads, value_rows, preferred_element_type=jnp.float32
        )
        row_dot = jnp.sum(attn_prob * prob_grad, -1, keepdims=True)
        score_grad = (attn_prob * (prob_grad - row_dot) * key_scale).astype(jnp.bfloat16)
        query_grad = jnp.einsum(
            "hnk,khe->nhe", score_grad, key_rows, preferred_element_type=jnp.float32
        )
        query_grad = query_grad.reshape(token_rows, model_width).astype(jnp.bfloat16)
        key_part = jnp.einsum(
            "hnk,nhe->khe", score_grad, query_heads, preferred_element_type=jnp.float32
        )
        prob_low = attn_prob.astype(jnp.bfloat16)
        value_part = jnp.einsum(
            "hnk,nhe->khe", prob_low, grad_heads, preferred_element_type=jnp.float32
        )
        keyval_part = jnp.concatenate(
            [
                key_part.reshape(block_total, token_rows, model_width),
                value_part.reshape(block_total, token_rows, model_width),
            ],
            -1,
        )
        remote = keyval_part[1:]
        summed = keyval_part[0]
        pick_now = take_tick(slot_pick, micro_index)
        for place_no, offset in enumerate(offsets):
            chosen_part = jnp.sum(jnp.where(pick_now[:, place_no, None, None], remote, 0.0), 0)
            returned = from_behind(chosen_part.astype(jnp.bfloat16), "view", offset)
            summed = summed + returned.astype(jnp.float32)
        proj_grad = jnp.concatenate([query_grad, summed.astype(jnp.bfloat16)], -1)
        normed_grad = jnp.einsum(
            "nf,df->nd", proj_grad, weight_in, preferred_element_type=jnp.float32
        )
        unit_rows = section_input.astype(jnp.float32) * factor
        inner = jnp.mean(normed_grad * unit_rows, -1, keepdims=True)
        input_grad = (
            out_grad.astype(jnp.float32) + factor * (normed_grad - unit_rows * inner)
        ).astype(jnp.bfloat16)
        incoming_grad = from_behind_2(input_grad, "section", -1)
        grad_list.append(input_grad)
        proj_list.append(proj_grad)
        outgrad_list.append(out_grad)
    back_start = section_total - 1 - section_no
    outputs_now = lax.dynamic_slice_in_dim(jnp.stack(output_list), section_no, micro_total, 0)
    grads_now = lax.dynamic_slice_in_dim(jnp.stack(grad_list), back_start, micro_total, 0)
    normed_all = lax.dynamic_slice_in_dim(
        jnp.stack(normed_list), section_no, micro_total, 0
    ).reshape(-1, model_width)
    attended_all = lax.dynamic_slice_in_dim(
        jnp.stack(attended_list), section_no, micro_total, 0
    ).reshape(-1, model_width)
    proj_all = lax.dynamic_slice_in_dim(jnp.stack(proj_list), back_start, micro_total, 0).reshape(
        -1, 3 * model_width
    )
    outgrad_all = lax.dynamic_slice_in_dim(
        jnp.stack(outgrad_list), back_start, micro_total, 0
    ).reshape(-1, model_width)
    share = 1.0 / (micro_total * lax.axis_size("dp"))
    grad_in, grad_out = weight_grads(normed_all, attended_all, proj_all, outgrad_all, share)
    section_outputs = outputs_now.reshape(1, micro_total, 1, token_rows, model_width)
    input_grads = grads_now.reshape(1, micro_total, 1, token_rows, model_width)
    return (section_outputs, input_grads, grad_in[None], grad_out[None])


def solution(mesh):
    in_specs = (
        P("dp", "view", None, None),
        P("dp", "view", None),
        P("dp", "view"),
        P("section", None, None),
        P("section", None, None),
        P("dp", "view", None, None),
    )
    out_specs = (
        P("section", "dp", "view", None, None),
        P("section", "dp", "view", None, None),
        P("section", ("view", "dp"), None),
        P("section", ("view", "dp"), None),
    )
    return jax.shard_map(
        on_device, mesh=mesh, in_specs=in_specs, out_specs=out_specs, check_vma=False
    )
```

```python
import functools
import math

import jax
import jax.numpy as jnp
from jax import lax
from jax.experimental import pallas as pl
from jax.experimental.pallas import tpu as pltpu
from jax.sharding import PartitionSpec as P

HEAD_DIM = 128
EPSILON = 1e-06
NEGATIVE = -1e30
MESH = pl.DeviceIdType.MESH
CHUNK = 512
PAIRS = ((6, 7), (0, 1), (2, 3), (4, 5))


def wgrad_kernel(
    share, nT, aT, proj, og, gin, gout,
    nT_r, aT_r, proj_r, og_r, G, r1, r2, r3, r4, r5,
    xs, xr, ss, rs,
):
    view = lax.axis_index("view")
    zi = lax.axis_index("dp")
    core = lax.rem(view, 2)
    yi = lax.rem(view // 2, 4)
    xi = view // 8
    peer = xi * 8 + yi * 2 + (1 - core)
    across = (1 - xi) * 8 + yi * 2 + core

    def y_dev(step):
        return {"view": xi * 8 + lax.rem(yi + step + 4, 4) * 2 + core}

    def z_dev(step):
        return {"dp": lax.rem(zi + step + 4, 4)}

    barrier = pltpu.get_barrier_semaphore()
    partners = ({"view": peer}, {"view": across}, y_dev(1), y_dev(-1), z_dev(1), z_dev(-1))
    for dev in partners:
        pl.semaphore_signal(barrier, inc=1, device_id=dev, device_id_type=MESH)
    pl.semaphore_wait(barrier, len(partners))

    def remote(src, dst, s, r, dev):
        return pltpu.make_async_remote_copy(
            src_ref=src, dst_ref=dst, send_sem=s, recv_sem=r, device_id=dev, device_id_type=MESH
        )

    def cols(ref, k):
        return ref.at[:, pl.ds(k * CHUNK, CHUNK)]

    pieces = {}
    pieces["a"] = remote(aT.at[:, 1 - core], aT_r, xs.at[8], xr.at[8], {"view": peer})
    pieces["n"] = remote(nT.at[:, 1 - core], nT_r, xs.at[9], xr.at[9], {"view": peer})
    for n in range(6):
        pieces[n] = remote(cols(proj, n), cols(proj_r, n), xs.at[n], xr.at[n], {"view": peer})
    for n in range(6, 8):
        pieces[n] = remote(
            cols(og, n - 6), cols(og_r, n - 6), xs.at[n], xr.at[n], {"view": peer}
        )
    for key in ("a", 6, 7, "n", 0, 1, 2, 3, 4, 5):
        pieces[key].start()

    def first(n, x_at, a):
        return G.at[n, x_at, a] if n % 2 == 0 else G.at[n, x_at, :, a]

    def second(n, x_at, a, b):
        return G.at[n, x_at, a, b] if n % 2 == 0 else G.at[n, x_at, b, a]

    whole = slice(None)
    sent = []

    def send(n, k, src, dst, dev):
        copy = remote(src, dst, ss.at[n, k], rs.at[n, k], dev)
        copy.start()
        sent.append(copy)
        return copy

    arrived = {}

    def add_into(ref, *others):
        total = ref[...].astype(jnp.float32)
        for other in others:
            total = total + other[...].astype(jnp.float32)
        ref[...] = total.astype(jnp.bfloat16)

    seen = set()

    def need(key):
        if key not in seen:
            seen.add(key)
            pieces[key].wait_recv()

    def stage(n, s):
        a, b = (yi, zi) if n % 2 == 0 else (zi, yi)
        dev1, dev2 = (y_dev, z_dev) if n % 2 == 0 else (z_dev, y_dev)
        if s == 0:
            if n >= 6:
                need("a")
                left, left_r, right, right_r, k = aT, aT_r, og, og_r, n - 6
            else:
                need("n")
                left, left_r, right, right_r, k = nT, nT_r, proj, proj_r, n
            need(n)
            rows = left.shape[0] * left.shape[2]
            toks = left.shape[3]
            mine = left[:, core].reshape(rows, toks)
            theirs = left_r[...].reshape(rows, toks)
            part = jnp.dot(
                mine, right[:, k * CHUNK : (k + 1) * CHUNK], preferred_element_type=jnp.float32
            ) + jnp.dot(
                theirs, right_r[:, k * CHUNK : (k + 1) * CHUNK], preferred_element_type=jnp.float32
            )
            G[n] = part.astype(jnp.bfloat16).reshape(G.shape[1:])
            opp = lax.rem(a + 2, 4)
            arrived[n, 0] = (
                send(n, 0, first(n, 0, opp), r1.at[n, 0], dev1(1)),
                send(n, 1, first(n, 1, opp), r1.at[n, 1], dev1(-1)),
            )
            return
        for copy in arrived[n, s - 1]:
            copy.wait_recv()
        if s == 1:
            up, down = lax.rem(a + 1, 4), lax.rem(a + 3, 4)
            add_into(first(n, 0, up), r1.at[n, 0])
            add_into(first(n, 1, down), r1.at[n, 1])
            arrived[n, 1] = (
                send(n, 2, first(n, whole, up), r2.at[n, 0], dev1(1)),
                send(n, 3, first(n, whole, down), r2.at[n, 1], dev1(-1)),
            )
        elif s == 2:
            add_into(first(n, whole, a), r2.at[n, 0], r2.at[n, 1])
            opp = lax.rem(b + 2, 4)
            arrived[n, 2] = (
                send(n, 4, second(n, 0, a, opp), r3.at[n, 0], dev2(1)),
                send(n, 5, second(n, 1, a, opp), r3.at[n, 1], dev2(-1)),
            )
        elif s == 3:
            up, down = lax.rem(b + 1, 4), lax.rem(b + 3, 4)
            add_into(second(n, 0, a, up), r3.at[n, 0])
            add_into(second(n, 1, a, down), r3.at[n, 1])
            arrived[n, 3] = (
                send(n, 6, second(n, whole, a, up), r4.at[n, 0], dev2(1)),
                send(n, 7, second(n, whole, a, down), r4.at[n, 1], dev2(-1)),
            )
        elif s == 4:
            add_into(second(n, whole, a, b), r4.at[n, 0], r4.at[n, 1])
            arrived[n, 4] = (
                send(n, 8, second(n, 1 - xi, a, b), r5.at[n], {"view": across}),
            )
        else:
            total = second(n, xi, a, b)[...].astype(jnp.float32) + r5[n].astype(jnp.float32)
            out, k = (gin, n) if n < 6 else (gout, n - 6)
            out[:, k * CHUNK : (k + 1) * CHUNK] = total * share

    stages = 6
    for turn in range(len(PAIRS) + stages - 1):
        for p in range(len(PAIRS)):
            s = turn - p
            if 0 <= s < stages:
                for n in PAIRS[p]:
                    stage(n, s)
    for copy in list(pieces.values()) + sent:
        copy.wait_send()


def weight_grads(nT, aT, proj, outgrad, share):
    toks, width = outgrad.shape
    chunks = 4 * width // CHUNK
    rows = width // 64
    vm = pl.BlockSpec(memory_space=pltpu.VMEM)
    bf = jnp.bfloat16
    return pl.pallas_call(
        functools.partial(wgrad_kernel, share),
        out_shape=(
            jax.ShapeDtypeStruct((rows, 3 * width), jnp.float32),
            jax.ShapeDtypeStruct((rows, width), jnp.float32),
        ),
        in_specs=[vm] * 4,
        out_specs=(vm, vm),
        scratch_shapes=[
            pltpu.VMEM((8, width // 16, toks), bf),
            pltpu.VMEM((8, width // 16, toks), bf),
            pltpu.VMEM((toks, 3 * width), bf),
            pltpu.VMEM((toks, width), bf),
            pltpu.VMEM((chunks, 2, 4, 4, rows, CHUNK), bf),
            pltpu.VMEM((chunks, 2, 4, rows, CHUNK), bf),
            pltpu.VMEM((chunks, 2, 2, 4, rows, CHUNK), bf),
            pltpu.VMEM((chunks, 2, rows, CHUNK), bf),
            pltpu.VMEM((chunks, 2, 2, rows, CHUNK), bf),
            pltpu.VMEM((chunks, rows, CHUNK), bf),
            pltpu.SemaphoreType.DMA((10,)),
            pltpu.SemaphoreType.DMA((10,)),
            pltpu.SemaphoreType.DMA((chunks, 9)),
            pltpu.SemaphoreType.DMA((chunks, 9)),
        ],
        compiler_params=pltpu.CompilerParams(
            collective_id=1, has_side_effects=True, vmem_limit_bytes=40 * 1024 * 1024
        ),
        cost_estimate=pl.CostEstimate(
            flops=2 * 512 * 512 * 4096, bytes_accessed=4 << 20, transcendentals=0
        ),
    )(nT, aT, proj, outgrad)


def ticks_kernel(
    scale,
    x_ref, cot_ref, live_ref, win_hbm, wout_hbm,
    out_ref, grad_ref, nT_ref, aT_ref, proj_ref, og_ref,
    win, wout, X, N, Q, KV, PR, AT, FA, AG, OWN, SP, RP,
    wsem, s_x, r_x, s_hop, r_hop, s_p, r_p,
):
    sec = lax.axis_index("section")
    view = lax.axis_index("view")
    views = lax.axis_size("view")
    core = lax.rem(view, 2)
    peer = {"view": view + 1 - 2 * core}
    ahead = {"view": lax.rem(view + 2, views)}
    behind = {"view": lax.rem(view + views - 2, views)}
    other = {"section": 1 - sec}
    micros, toks, width = x_ref.shape
    heads = width // HEAD_DIM
    relay = 3 - core
    straight = 2 + core
    tile = 512
    f32, bf = jnp.float32, jnp.bfloat16

    loads = [
        pltpu.make_async_copy(win_hbm, win, wsem.at[0]),
        pltpu.make_async_copy(wout_hbm, wout, wsem.at[1]),
    ]
    for load in loads:
        load.start()

    barrier = pltpu.get_barrier_semaphore()
    for dev in (peer, ahead, behind, other):
        pl.semaphore_signal(barrier, inc=1, device_id=dev, device_id_type=MESH)
    pl.semaphore_wait(barrier, 4)

    def remote(src, dst, s, r, dev):
        return pltpu.make_async_remote_copy(
            src_ref=src, dst_ref=dst, send_sem=s, recv_sem=r, device_id=dev, device_id_type=MESH
        )

    def spread(m):
        return [
            remote(X.at[m, 0], X.at[m, 1], s_x.at[m, 0], r_x.at[m, 0], peer),
            remote(X.at[m, 0], X.at[m, 2], s_x.at[m, 1], r_x.at[m, 1], ahead),
            remote(X.at[m, 0], X.at[m, 3], s_x.at[m, 2], r_x.at[m, 2], behind),
        ]

    def pass_on(m):
        return remote(X.at[m, relay], X.at[m, 4], s_x.at[m, 3], r_x.at[m, 3], peer)

    def hop_out(m):
        return remote(out_ref.at[m], X.at[m, 0], s_hop.at[m], r_hop.at[m], other)

    def hop_back(m):
        return remote(grad_ref.at[m], og_ref.at[m], s_hop.at[m], r_hop.at[m], other)

    def parts(m):
        return {
            "diag": remote(SP.at[m, 3], RP.at[m, 3], s_p.at[m, 3], r_p.at[m, 3], peer),
            "peer": remote(SP.at[m, 0], RP.at[m, 0], s_p.at[m, 0], r_p.at[m, 0], peer),
            "behind": remote(SP.at[m, 1], RP.at[m, 1], s_p.at[m, 1], r_p.at[m, 1], behind),
            "ahead": remote(SP.at[m, 2], RP.at[m, 2], s_p.at[m, 2], r_p.at[m, 2], ahead),
        }

    def start_spread(m):
        for copy in spread(m):
            copy.start()

    @pl.when(sec == 0)
    def _():
        for m in range(micros):
            X[m, 0] = x_ref[m]
            start_spread(m)

    @pl.when(sec == 1)
    def _():
        for m in range(micros):
            og_ref[m] = cot_ref[m]

    def norm_block(m, k):
        rows = X[m, k].astype(f32)
        factor = lax.rsqrt(jnp.mean(rows * rows, -1, keepdims=True) + EPSILON)
        normed = (rows * factor).astype(bf)
        N[k] = normed
        return factor, normed

    def project(m, k0, k1):
        rows = (k1 - k0) * toks
        left = N.at[pl.ds(k0, k1 - k0)]

        @pl.loop(0, 2 * width // tile)
        def _(j):
            at = pl.multiple_of(j * tile, tile)
            block = jnp.dot(
                left[...].reshape(rows, width),
                win[:, pl.ds(width + at, tile)],
                preferred_element_type=f32,
            ).astype(bf)
            KV[m, k0 * toks : k1 * toks, pl.ds(at, tile)] = block

    def forward(m):
        @pl.when(sec == 1)
        def _():
            if m == 0:
                hop_out(m).wait_recv()
                start_spread(m)

        copies = spread(m)
        factor, normed = norm_block(m, 0)
        FA[m] = factor
        nT_ref[:, :, :, m * toks : (m + 1) * toks] = normed.T.reshape(
            8, 2, width // 16, toks
        )
        if m == 0:
            loads[0].wait()

        @pl.loop(0, width // tile)
        def _(j):
            at = pl.multiple_of(j * tile, tile)
            Q[m, :, pl.ds(at, tile)] = jnp.dot(
                N[0], win[:, pl.ds(at, tile)], preferred_element_type=f32
            ).astype(bf)

        copies[0].wait_recv()
        norm_block(m, 1)
        project(m, 0, 2)
        copies[1].wait_recv()
        copies[2].wait_recv()
        pass_on(m).start()
        norm_block(m, 2)
        norm_block(m, 3)
        project(m, 2, 4)
        pass_on(m).wait_recv()
        norm_block(m, 4)
        project(m, 4, 5)
        if m == 0:
            @pl.when(sec == 1)
            def _():
                hop_out(1).wait_recv()
                start_spread(1)

        live = live_ref[m] > 0.0

        def head(h, carry):
            at = pl.multiple_of(h * HEAD_DIM, HEAD_DIM)
            cols = pl.ds(at, HEAD_DIM)
            scores = lax.dot_general(
                Q[m, :, cols], KV[m, :, cols], (((1,), (1,)), ((), ())),
                preferred_element_type=f32,
            ) * scale
            masked = jnp.where(live, scores, NEGATIVE)
            terms = jnp.exp(masked - jnp.max(masked, -1, keepdims=True))
            prob = terms * (1.0 / jnp.sum(terms, -1, keepdims=True))
            PR[m, h] = prob
            AT[m, :, cols] = jnp.dot(
                prob.astype(bf), KV[m, :, pl.ds(width + at, HEAD_DIM)],
                preferred_element_type=f32,
            ).astype(bf)
            return carry

        lax.fori_loop(0, heads, head, 0, unroll=2)
        if m == 0:
            loads[1].wait()

        @pl.loop(0, width // tile)
        def _(j):
            cols = pl.ds(pl.multiple_of(j * tile, tile), tile)
            branch = jnp.dot(AT[m], wout[:, cols], preferred_element_type=f32)
            out_ref[m, :, cols] = (X[m, 0, :, cols].astype(f32) + branch).astype(bf)

        @pl.when(sec == 0)
        def _():
            hop_out(m).start()

        aT_ref[:, :, :, m * toks : (m + 1) * toks] = AT[m].T.reshape(8, 2, width // 16, toks)

    def backward(m):
        @pl.when(sec == 0)
        def _():
            hop_back(m).wait_recv()

        @pl.loop(0, width // tile)
        def _(j):
            at = pl.multiple_of(j * tile, tile)
            AG[:, pl.ds(at, tile)] = lax.dot_general(
                og_ref[m], wout[pl.ds(at, tile)], (((1,), (1,)), ((), ())),
                preferred_element_type=f32,
            ).astype(bf)

        def head(h, carry):
            at = pl.multiple_of(h * HEAD_DIM, HEAD_DIM)
            cols = pl.ds(at, HEAD_DIM)
            vcols = pl.ds(width + at, HEAD_DIM)
            gh = AG[:, cols]
            prob = PR[m, h]
            prob_grad = lax.dot_general(
                gh, KV[m, :, vcols], (((1,), (1,)), ((), ())), preferred_element_type=f32
            )
            row_dot = jnp.sum(prob * prob_grad, -1, keepdims=True)
            score_grad = (prob * (prob_grad - row_dot) * scale).astype(bf)
            proj_ref[m, :, cols] = jnp.dot(
                score_grad, KV[m, :, cols], preferred_element_type=f32
            ).astype(bf)
            key_part = lax.dot_general(
                score_grad, Q[m, :, cols], (((0,), (0,)), ((), ())), preferred_element_type=f32
            )
            value_part = lax.dot_general(
                prob.astype(bf), gh, (((0,), (0,)), ((), ())), preferred_element_type=f32
            )
            OWN[m, :, cols] = key_part[:toks]
            OWN[m, :, vcols] = value_part[:toks]
            for k in range(4):
                SP[m, k, :, cols] = key_part[(k + 1) * toks : (k + 2) * toks].astype(bf)
                SP[m, k, :, vcols] = value_part[(k + 1) * toks : (k + 2) * toks].astype(bf)
            return carry

        lax.fori_loop(0, heads, head, 0, unroll=2)
        copies = parts(m)
        copies["diag"].start()

        @pl.when(core == 0)
        def _():
            copies["behind"].start()

        @pl.when(core == 1)
        def _():
            copies["ahead"].start()

        copies["peer"].start()
        copies["diag"].wait_recv()
        SP[m, relay - 1] = (
            SP[m, relay - 1].astype(f32) + RP[m, 3].astype(f32)
        ).astype(bf)

        @pl.when(core == 0)
        def _():
            copies["ahead"].start()

        @pl.when(core == 1)
        def _():
            copies["behind"].start()

    def finish(m):
        copies = parts(m)
        for name in ("peer", "behind", "ahead"):
            copies[name].wait_recv()
        total = OWN[m]
        for k in range(3):
            total = total + RP[m, k].astype(f32)
        proj_ref[m, :, width:] = total.astype(bf)

        @pl.loop(0, width // tile)
        def _(j):
            at = pl.multiple_of(j * tile, tile)
            OWN[m, :, pl.ds(at, tile)] = lax.dot_general(
                proj_ref[m], win[pl.ds(at, tile)], (((1,), (1,)), ((), ())),
                preferred_element_type=f32,
            )

        normed_grad = OWN[m, :, :width]
        factor = FA[m]
        unit = X[m, 0].astype(f32) * factor
        inner = jnp.mean(normed_grad * unit, -1, keepdims=True)
        grad_ref[m] = (
            og_ref[m].astype(f32) + factor * (normed_grad - unit * inner)
        ).astype(bf)

        @pl.when(sec == 1)
        def _():
            hop_back(m).start()

    for m in range(micros):
        forward(m)
    for m in range(micros):
        backward(m)
    for m in range(micros):
        finish(m)

    for m in range(micros):
        for copy in spread(m) + [pass_on(m)] + list(parts(m).values()):
            copy.wait_send()

        @pl.when(sec == 0)
        def _():
            hop_out(m).wait_send()

        @pl.when(sec == 1)
        def _():
            hop_back(m).wait_send()


def run_ticks(x, cot, live, w_in, w_out):
    micros, toks, width = x.shape
    heads = width // HEAD_DIM
    blocks = 5
    vm = pl.BlockSpec(memory_space=pltpu.VMEM)
    hbm = pl.BlockSpec(memory_space=pl.ANY)
    bf, f32 = jnp.bfloat16, jnp.float32
    sds = jax.ShapeDtypeStruct
    dma = pltpu.SemaphoreType.DMA
    return pl.pallas_call(
        functools.partial(ticks_kernel, 1.0 / math.sqrt(HEAD_DIM)),
        out_shape=(
            sds((micros, toks, width), bf),
            sds((micros, toks, width), bf),
            sds((8, 2, width // 16, micros * toks), bf),
            sds((8, 2, width // 16, micros * toks), bf),
            sds((micros, toks, 3 * width), bf),
            sds((micros, toks, width), bf),
        ),
        in_specs=[vm, vm, vm, hbm, hbm],
        out_specs=(vm,) * 6,
        scratch_shapes=[
            pltpu.VMEM((width, 3 * width), bf),
            pltpu.VMEM((width, width), bf),
            pltpu.VMEM((micros, blocks, toks, width), bf),
            pltpu.VMEM((blocks, toks, width), bf),
            pltpu.VMEM((micros, toks, width), bf),
            pltpu.VMEM((micros, blocks * toks, 2 * width), bf),
            pltpu.VMEM((micros, heads, toks, blocks * toks), f32),
            pltpu.VMEM((micros, toks, width), bf),
            pltpu.VMEM((micros, toks, 1), f32),
            pltpu.VMEM((toks, width), bf),
            pltpu.VMEM((micros, toks, 2 * width), f32),
            pltpu.VMEM((micros, 4, toks, 2 * width), bf),
            pltpu.VMEM((micros, 4, toks, 2 * width), bf),
            dma((2,)),
            dma((micros, 4)), dma((micros, 4)),
            dma((micros,)), dma((micros,)),
            dma((micros, 4)), dma((micros, 4)),
        ],
        compiler_params=pltpu.CompilerParams(
            collective_id=2, has_side_effects=True, vmem_limit_bytes=56 * 1024 * 1024
        ),
        cost_estimate=pl.CostEstimate(
            flops=20 * 10**9, bytes_accessed=12 << 20, transcendentals=2 * 10**6
        ),
    )(x, cot, live, w_in, w_out)


def on_device(scenes, neighbours, counts, w_in, w_out, cotangent):
    views = lax.axis_size("view")
    micros, _, toks, width = scenes.shape
    slots = neighbours.shape[2]
    view = lax.axis_index("view")
    core = view % 2
    side = 1 - 2 * core
    offsets = jnp.stack([0 * core, side, -2 + 0 * core, 2 + 0 * core, -side])
    slot_live = jnp.arange(slots, dtype=jnp.int32)[None, :] < counts
    rel = (neighbours[:, 0, :] - view) % views
    hit = (rel[:, :, None] == (offsets % views)[None, None, :]) & slot_live[:, :, None]
    block_live = jnp.any(hit, 1).at[:, 0].set(True)
    live = jnp.repeat(block_live.astype(jnp.float32), toks, axis=1)[:, None, :]
    share = 1.0 / (micros * lax.axis_size("dp"))
    outputs, grads, nT, aT, proj, outgrad = run_ticks(
        scenes[:, 0], cotangent[:, 0], live, w_in[0], w_out[0]
    )
    grad_in, grad_out = weight_grads(
        nT, aT, proj.reshape(-1, 3 * width), outgrad.reshape(-1, width), share
    )
    return (outputs[None, :, None], grads[None, :, None], grad_in[None], grad_out[None])


def solution(mesh):
    in_specs = (
        P("dp", "view", None, None),
        P("dp", "view", None),
        P("dp", "view"),
        P("section", None, None),
        P("section", None, None),
        P("dp", "view", None, None),
    )
    out_specs = (
        P("section", "dp", "view", None, None),
        P("section", "dp", "view", None, None),
        P("section", ("view", "dp"), None),
        P("section", ("view", "dp"), None),
    )
    return jax.shard_map(
        on_device, mesh=mesh, in_specs=in_specs, out_specs=out_specs, check_vma=False
    )
```

```python
import functools
import math

import jax
import jax.numpy as jnp
from jax import lax
from jax.experimental import pallas as pl
from jax.experimental.pallas import tpu as pltpu
from jax.sharding import PartitionSpec as P

HEAD_DIM = 128
EPSILON = 1e-06
NEGATIVE = -1e30
MESH = pl.DeviceIdType.MESH
CHUNK = 512
PAIRS = ((6, 7), (0, 1), (2, 3), (4, 5))
STAGES = 6
PIECES = 4
BLOCKS = 5
LAST = (((1,), (1,)), ((), ()))


def scene_kernel(
    scale, share,
    x_ref, cot_ref, nbr_ref, cnt_ref, win_hbm, wout_hbm,
    out_ref, grad_ref, gin, gout,
    win, wout, X, OG, N, QKV, AG, PR, AT, FA, ST, SS, RD, NG,
    LN, LA, SN, SA, RP, RO, G, r1, r2, r3, r4, r5,
    wsem, s_sp, r_sp, s_h, r_h, s_q, r_q, s_a, r_a, s_st, r_st, s_rd, r_rd,
    s_l, r_l, s_o, r_o, s_pj, r_pj, ss, rs,
):
    sec = lax.axis_index("section")
    view = lax.axis_index("view")
    zi = lax.axis_index("dp")
    core = lax.rem(view, 2)
    yi = lax.rem(view // 2, 4)
    xi = view // 8
    micros, toks, width = x_ref.shape
    heads = width // HEAD_DIM
    relay = 3 - core
    f32, bf = jnp.float32, jnp.bfloat16

    peer = {"view": view + 1 - 2 * core}
    ahead = {"view": lax.rem(view + 2, 16)}
    behind = {"view": lax.rem(view + 14, 16)}
    diag = {"view": lax.rem(view + 15 + 2 * core, 16)}
    other = {"section": 1 - sec}
    across = {"view": lax.rem(view + 8, 16)}

    def y_dev(step):
        return {"view": xi * 8 + lax.rem(yi + step + 4, 4) * 2 + core}

    def z_dev(step):
        return {"dp": lax.rem(zi + step + 4, 4)}

    loads = [
        pltpu.make_async_copy(win_hbm, win, wsem.at[0]),
        pltpu.make_async_copy(wout_hbm, wout, wsem.at[1]),
    ]
    for load in loads:
        load.start()

    partners = (
        peer, ahead, behind, diag, other, across, y_dev(1), y_dev(-1), z_dev(1), z_dev(-1)
    )
    barrier = pltpu.get_barrier_semaphore()
    for dev in partners:
        pl.semaphore_signal(barrier, inc=1, device_id=dev, device_id_type=MESH)
    pl.semaphore_wait(barrier, len(partners))

    def remote(src, dst, s, r, dev):
        return pltpu.make_async_remote_copy(
            src_ref=src, dst_ref=dst, send_sem=s, recv_sem=r, device_id=dev, device_id_type=MESH
        )

    def when_section(s):
        return pl.when(sec == s)

    step = toks // PIECES

    def spread(t, m, way, i):
        buf = (X, OG)[t]
        rows = pl.ds(i * step, step)
        return remote(
            buf.at[m, 0, rows], buf.at[m, 1 + way, rows],
            s_sp.at[t, m, way, i], r_sp.at[t, m, way, i], (ahead, behind)[way],
        )

    def hop(t, m, i):
        src, dst = ((out_ref, X), (grad_ref, OG))[t]
        rows = pl.ds(i * step, step)
        return remote(
            src.at[m, rows], dst.at[m, 0, rows], s_h.at[m, i], r_h.at[m, i], other
        )

    def share_qkv(m, which, j):
        src, dst = ((0, 1), (relay, 4))[which]
        cols = pl.ds(j * width, width)
        return remote(
            QKV.at[m, src, :, cols], QKV.at[m, dst, :, cols],
            s_q.at[m, which, j], r_q.at[m, which, j], peer,
        )

    def share_ag(m, which):
        src, dst = ((0, 1), (relay, 4))[which]
        return remote(AG.at[m, src], AG.at[m, dst], s_a.at[m, which], r_a.at[m, which], peer)

    ROUTES = {1: (1, peer), 3: (2, behind), 2: (3, ahead), 4: (4, diag)}

    def stats_to(m, block):
        target, dev = ROUTES[block]
        return remote(
            SS.at[m, target - 1], ST.at[m, block],
            s_st.at[m, block - 1], r_st.at[m, block - 1], dev,
        )

    def dots_to(m, block):
        return remote(
            RD.at[m, 0], RD.at[m, block],
            s_rd.at[m, block - 1], r_rd.at[m, block - 1], ROUTES[block][1],
        )

    own_toks = micros * toks

    def share_left(which):
        src, dst = ((SN, LN), (SA, LA))[which]
        return remote(
            src, dst.at[:, :, pl.ds(own_toks, own_toks)], s_l.at[which], r_l.at[which], peer
        )

    def share_og(m):
        return remote(RO.at[m], RO.at[micros + m], s_o.at[m], r_o.at[m], peer)

    def share_proj(m, which):
        cols = (pl.ds(0, width), pl.ds(width, 2 * width))[which]
        return remote(
            RP.at[m, :, cols], RP.at[micros + m, :, cols],
            s_pj.at[m, which], r_pj.at[m, which], peer,
        )

    def start_spread(t, m):
        for i in range(PIECES):
            spread(t, m, 0, i).start()
            spread(t, m, 1, i).start()

    def wait_spread(t, m):
        for i in range(PIECES):
            spread(t, m, 0, i).wait_recv()
            spread(t, m, 1, i).wait_recv()

    def receive_hop(t, m):
        for i in range(PIECES):
            hop(t, m, i).wait_recv()
            spread(t, m, 0, i).start()
            spread(t, m, 1, i).start()

    side = 1 - 2 * core
    offsets = (0, side, -2, 2, -side)

    def live_block(m, k):
        if k == 0:
            return jnp.ones((1, toks), f32)
        live = jnp.float32(0.0)
        for j in range(nbr_ref.shape[1]):
            rel = lax.rem(nbr_ref[m, j] - view - offsets[k] + 32, 16)
            hit = jnp.logical_and(rel == 0, j < cnt_ref[m, 0])
            live = jnp.where(hit, jnp.float32(1.0), live)
        return jnp.full((1, toks), live, f32)

    def norm_block(m, at):
        rows = X[m, at].astype(f32)
        factor = lax.rsqrt(jnp.mean(rows * rows, -1, keepdims=True) + EPSILON)
        normed = (rows * factor).astype(bf)
        N[at] = normed
        return factor, normed

    def keep_left(value, mine, theirs, m):
        parts = value.T.reshape(8, 2, width // 16, toks)
        cols = slice(m * toks, (m + 1) * toks)
        first, second = parts[:, 0], parts[:, 1]
        mine[:, :, cols] = jnp.where(core == 0, first, second)
        theirs[:, :, cols] = jnp.where(core == 0, second, first)

    def lanes():
        return lax.broadcasted_iota(jnp.int32, (toks, HEAD_DIM), 1)

    def forward(m):
        if m == 0:
            @when_section(1)
            def _():
                receive_hop(0, 0)

        factor, normed = norm_block(m, 0)
        FA[m] = factor
        for j in (1, 2, 0):
            cols = slice(j * width, (j + 1) * width)
            QKV[m, 0, :, cols] = jnp.dot(
                N[0], win[:, cols], preferred_element_type=f32
            ).astype(bf)
            share_qkv(m, 0, j).start()
        keep_left(normed, LN, SN, m)
        wait_spread(0, m)
        if m == 0:
            @when_section(0)
            def _():
                start_spread(0, 1)

        norm_block(m, 1)
        norm_block(m, 2)
        for j in (1, 2, 0):
            cols = slice(j * width, (j + 1) * width)
            near = jnp.dot(
                N[1:3].reshape(2 * toks, width), win[:, cols], preferred_element_type=f32
            ).astype(bf)
            QKV[m, 2:4, :, cols] = near.reshape(2, toks, width)
            share_qkv(m, 1, j).start()
        for j in (1, 2):
            share_qkv(m, 0, j).wait_recv()
            share_qkv(m, 1, j).wait_recv()
        lives = [live_block(m, k) for k in range(BLOCKS)]
        live = jnp.concatenate(lives, 1) > 0.0
        stats = jnp.zeros((toks, HEAD_DIM), f32)
        for h in range(heads):
            cols = slice(h * HEAD_DIM, (h + 1) * HEAD_DIM)
            kcols = slice(width + h * HEAD_DIM, width + (h + 1) * HEAD_DIM)
            vcols = slice(2 * width + h * HEAD_DIM, 2 * width + (h + 1) * HEAD_DIM)
            scores = lax.dot_general(
                QKV[m, 0, :, cols], QKV[m, :, :, kcols].reshape(BLOCKS * toks, HEAD_DIM), LAST,
                preferred_element_type=f32,
            ) * scale
            masked = jnp.where(live, scores, NEGATIVE)
            top = jnp.max(masked, -1, keepdims=True)
            terms = jnp.exp(masked - top)
            inverse = 1.0 / jnp.sum(terms, -1, keepdims=True)
            prob = terms * inverse
            PR[m, h] = prob
            AT[m, :, cols] = jnp.dot(
                prob.astype(bf), QKV[m, :, :, vcols].reshape(BLOCKS * toks, HEAD_DIM),
                preferred_element_type=f32,
            ).astype(bf)
            stats = jnp.where(lanes() == h, top, stats)
            stats = jnp.where(lanes() == heads + h, inverse, stats)
        if m == 0:
            @when_section(1)
            def _():
                receive_hop(0, 1)

            @when_section(0)
            def _():
                loads[1].wait()

        branch = jnp.dot(AT[m], wout[...], preferred_element_type=f32)
        out_ref[m] = (X[m, 0].astype(f32) + branch).astype(bf)

        @when_section(0)
        def _():
            for i in range(PIECES):
                hop(0, m, i).start()

        turned = stats.T
        ST[m, 0] = turned[: 2 * heads]
        for k in range(1, BLOCKS):
            SS[m, k - 1, :heads] = jnp.where(lives[k] > 0.0, turned[:heads], -NEGATIVE)
            SS[m, k - 1, heads:] = turned[heads : 2 * heads]
        for block in ROUTES:
            stats_to(m, block).start()
        keep_left(AT[m], LA, SA, m)

    def own_ag(m):
        AG[m, 0] = lax.dot_general(
            OG[m, 0], wout[...], LAST, preferred_element_type=f32
        ).astype(bf)
        share_ag(m, 0).start()

    def near_ag(m):
        wait_spread(1, m)
        near = lax.dot_general(
            OG[m, 1:3].reshape(2 * toks, width), wout[...], LAST, preferred_element_type=f32
        ).astype(bf)
        AG[m, 2:4] = near.reshape(2, toks, width)
        share_ag(m, 1).start()

    def backward(m):
        @when_section(0)
        def _():
            receive_hop(1, m)
            own_ag(m)

        RO[m] = OG[m, 0]
        share_og(m).start()
        dots = jnp.zeros((toks, HEAD_DIM), f32)
        for h in range(heads):
            cols = slice(h * HEAD_DIM, (h + 1) * HEAD_DIM)
            kcols = slice(width + h * HEAD_DIM, width + (h + 1) * HEAD_DIM)
            vcols = slice(2 * width + h * HEAD_DIM, 2 * width + (h + 1) * HEAD_DIM)
            prob = PR[m, h]
            prob_grad = lax.dot_general(
                AG[m, 0, :, cols], QKV[m, :, :, vcols].reshape(BLOCKS * toks, HEAD_DIM), LAST,
                preferred_element_type=f32,
            )
            row_dot = jnp.sum(prob * prob_grad, -1, keepdims=True)
            score_grad = (prob * (prob_grad - row_dot) * scale).astype(bf)
            RP[m, :, cols] = jnp.dot(
                score_grad, QKV[m, :, :, kcols].reshape(BLOCKS * toks, HEAD_DIM),
                preferred_element_type=f32,
            ).astype(bf)
            dots = jnp.where(lanes() == h, row_dot, dots)
        RD[m, 0] = dots.T[:heads]
        for block in ROUTES:
            dots_to(m, block).start()
        share_proj(m, 0).start()

        @when_section(0)
        def _():
            near_ag(m)

        for which in range(2):
            share_qkv(m, which, 0).wait_recv()
            share_ag(m, which).wait_recv()
        for block in ROUTES:
            stats_to(m, block).wait_recv()
            dots_to(m, block).wait_recv()

        def row(ref, h):
            return jnp.concatenate([ref[m, k, h : h + 1, :] for k in range(BLOCKS)], 1)

        for h in range(heads):
            cols = slice(h * HEAD_DIM, (h + 1) * HEAD_DIM)
            kcols = slice(width + h * HEAD_DIM, width + (h + 1) * HEAD_DIM)
            vcols = slice(2 * width + h * HEAD_DIM, 2 * width + (h + 1) * HEAD_DIM)
            queries = QKV[m, :, :, cols].reshape(BLOCKS * toks, HEAD_DIM)
            out_grads = AG[m, :, :, cols].reshape(BLOCKS * toks, HEAD_DIM)
            scores = lax.dot_general(
                QKV[m, 0, :, kcols], queries, LAST, preferred_element_type=f32
            ) * scale
            prob = jnp.exp(scores - row(ST, h)) * row(ST, heads + h)
            prob_grad = lax.dot_general(
                QKV[m, 0, :, vcols], out_grads, LAST, preferred_element_type=f32
            )
            score_grad = (prob * (prob_grad - row(RD, h)) * scale).astype(bf)
            RP[m, :, kcols] = jnp.dot(
                score_grad, queries, preferred_element_type=f32
            ).astype(bf)
            RP[m, :, vcols] = jnp.dot(
                prob.astype(bf), out_grads, preferred_element_type=f32
            ).astype(bf)
        share_proj(m, 1).start()

    def finish(m):
        half = width // 2
        for j in range(2):
            NG[:, j * half : (j + 1) * half] = lax.dot_general(
                RP[m], win[j * half : (j + 1) * half, :], LAST, preferred_element_type=f32
            )
        normed_grad = NG[...]
        factor = FA[m]
        unit = X[m, 0].astype(f32) * factor
        inner = jnp.mean(normed_grad * unit, -1, keepdims=True)
        grad_ref[m] = (
            OG[m, 0].astype(f32) + factor * (normed_grad - unit * inner)
        ).astype(bf)

    whole = slice(None)

    def first(n, x_at, a):
        return G.at[n, x_at, a] if n % 2 == 0 else G.at[n, x_at, :, a]

    def second(n, x_at, a, b):
        return G.at[n, x_at, a, b] if n % 2 == 0 else G.at[n, x_at, b, a]

    def ring(n, s):
        a, b = (yi, zi) if n % 2 == 0 else (zi, yi)
        dev1, dev2 = (y_dev, z_dev) if n % 2 == 0 else (z_dev, y_dev)

        def make(k, src, dst, dev):
            return remote(src, dst, ss.at[n, k], rs.at[n, k], dev)

        def turn(value, by):
            return lax.rem(value + by, 4)

        if s == 0:
            return (
                make(0, first(n, 0, turn(a, 2)), r1.at[n, 0], dev1(1)),
                make(1, first(n, 1, turn(a, 2)), r1.at[n, 1], dev1(-1)),
            )
        if s == 1:
            return (
                make(2, first(n, whole, turn(a, 1)), r2.at[n, 0], dev1(1)),
                make(3, first(n, whole, turn(a, 3)), r2.at[n, 1], dev1(-1)),
            )
        if s == 2:
            return (
                make(4, second(n, 0, a, turn(b, 2)), r3.at[n, 0], dev2(1)),
                make(5, second(n, 1, a, turn(b, 2)), r3.at[n, 1], dev2(-1)),
            )
        if s == 3:
            return (
                make(6, second(n, whole, a, turn(b, 1)), r4.at[n, 0], dev2(1)),
                make(7, second(n, whole, a, turn(b, 3)), r4.at[n, 1], dev2(-1)),
            )
        return (make(8, second(n, 1 - xi, a, b), r5.at[n], across),)

    def add_into(ref, *others):
        total = ref[...].astype(f32)
        for item in others:
            total = total + item[...].astype(f32)
        ref[...] = total.astype(bf)

    def stage(n, s):
        a, b = (yi, zi) if n % 2 == 0 else (zi, yi)
        if s > 0:
            for copy in ring(n, s - 1):
                copy.wait_recv()
        if s == 0:
            left = LA if n >= 6 else LN
            right, k = (RO, n - 6) if n >= 6 else (RP, n)
            part = jnp.dot(
                left[...].reshape(left.shape[0] * left.shape[1], 2 * own_toks),
                right[:, :, k * CHUNK : (k + 1) * CHUNK].reshape(2 * own_toks, CHUNK),
                preferred_element_type=f32,
            )
            G[n] = part.astype(bf).reshape(G.shape[1:])
        elif s == 1:
            add_into(first(n, 0, lax.rem(a + 1, 4)), r1.at[n, 0])
            add_into(first(n, 1, lax.rem(a + 3, 4)), r1.at[n, 1])
        elif s == 2:
            add_into(first(n, whole, a), r2.at[n, 0], r2.at[n, 1])
        elif s == 3:
            add_into(second(n, 0, a, lax.rem(b + 1, 4)), r3.at[n, 0])
            add_into(second(n, 1, a, lax.rem(b + 3, 4)), r3.at[n, 1])
        elif s == 4:
            add_into(second(n, whole, a, b), r4.at[n, 0], r4.at[n, 1])
        else:
            total = second(n, xi, a, b)[...].astype(f32) + r5[n].astype(f32)
            out, k = (gin, n) if n < 6 else (gout, n - 6)
            out[:, k * CHUNK : (k + 1) * CHUNK] = total * share
        if s < STAGES - 1:
            for copy in ring(n, s):
                copy.start()

    @when_section(0)
    def _():
        for m in range(micros):
            X[m, 0] = x_ref[m]
        start_spread(0, 0)

    @when_section(1)
    def _():
        for m in range(micros):
            OG[m, 0] = cot_ref[m]
            start_spread(1, m)

    loads[0].wait()

    @when_section(1)
    def _():
        loads[1].wait()
        for m in range(micros):
            own_ag(m)
            near_ag(m)

    for m in range(micros):
        forward(m)
    for which in range(2):
        share_left(which).start()
    for m in range(micros):
        backward(m)

        @when_section(1)
        def _():
            finish(m)
            for i in range(PIECES):
                hop(1, m, i).start()

    for m in range(micros):
        share_og(m).wait_recv()
    share_left(1).wait_recv()
    for turn in range(len(PAIRS) + STAGES - 1):
        for p in range(len(PAIRS)):
            s = turn - p
            if p == 1 and s == 0:
                share_left(0).wait_recv()
                for m in range(micros):
                    share_proj(m, 0).wait_recv()
            if p == 2 and s == 0:
                for m in range(micros):
                    share_proj(m, 1).wait_recv()
            if 0 <= s < STAGES:
                for n in PAIRS[p]:
                    stage(n, s)
        if turn in (2, 3):
            @when_section(0)
            def _():
                finish(turn - 2)

    for m in range(micros):
        for t in range(2):
            for i in range(PIECES):
                spread(t, m, 0, i).wait_send()
                spread(t, m, 1, i).wait_send()
        for i in range(PIECES):
            @when_section(0)
            def _():
                hop(0, m, i).wait_send()

            @when_section(1)
            def _():
                hop(1, m, i).wait_send()
        for which in range(2):
            for j in range(3):
                share_qkv(m, which, j).wait_send()
            share_ag(m, which).wait_send()
            share_proj(m, which).wait_send()
        for block in ROUTES:
            stats_to(m, block).wait_send()
            dots_to(m, block).wait_send()
        share_og(m).wait_send()
    for which in range(2):
        share_left(which).wait_send()
    for pair in PAIRS:
        for n in pair:
            for s in range(STAGES - 1):
                for copy in ring(n, s):
                    copy.wait_send()


def on_device(scenes, neighbours, counts, w_in, w_out, cotangent):
    micros, _, toks, width = scenes.shape
    heads = width // HEAD_DIM
    share = 1.0 / (micros * lax.axis_size("dp"))
    chunks = 4 * width // CHUNK
    rows = width // 64
    group = width // 16
    vm = pl.BlockSpec(memory_space=pltpu.VMEM)
    sm = pl.BlockSpec(memory_space=pltpu.SMEM)
    hbm = pl.BlockSpec(memory_space=pl.ANY)
    bf, f32 = jnp.bfloat16, jnp.float32
    sds = jax.ShapeDtypeStruct
    dma = pltpu.SemaphoreType.DMA
    outputs, grads, grad_in, grad_out = pl.pallas_call(
        functools.partial(scene_kernel, 1.0 / math.sqrt(HEAD_DIM), share),
        out_shape=(
            sds((micros, toks, width), bf),
            sds((micros, toks, width), bf),
            sds((rows, 3 * width), f32),
            sds((rows, width), f32),
        ),
        in_specs=[vm, vm, sm, sm, hbm, hbm],
        out_specs=(vm,) * 4,
        scratch_shapes=[
            pltpu.VMEM((width, 3 * width), bf),
            pltpu.VMEM((width, width), bf),
            pltpu.VMEM((micros, 3, toks, width), bf),
            pltpu.VMEM((micros, 3, toks, width), bf),
            pltpu.VMEM((3, toks, width), bf),
            pltpu.VMEM((micros, BLOCKS, toks, 3 * width), bf),
            pltpu.VMEM((micros, BLOCKS, toks, width), bf),
            pltpu.VMEM((micros, heads, toks, BLOCKS * toks), f32),
            pltpu.VMEM((micros, toks, width), bf),
            pltpu.VMEM((micros, toks, 1), f32),
            pltpu.VMEM((micros, BLOCKS, 2 * heads, toks), f32),
            pltpu.VMEM((micros, BLOCKS - 1, 2 * heads, toks), f32),
            pltpu.VMEM((micros, BLOCKS, heads, toks), f32),
            pltpu.VMEM((toks, width), f32),
            pltpu.VMEM((8, group, 2 * micros * toks), bf),
            pltpu.VMEM((8, group, 2 * micros * toks), bf),
            pltpu.VMEM((8, group, micros * toks), bf),
            pltpu.VMEM((8, group, micros * toks), bf),
            pltpu.VMEM((2 * micros, toks, 3 * width), bf),
            pltpu.VMEM((2 * micros, toks, width), bf),
            pltpu.VMEM((chunks, 2, 4, 4, rows, CHUNK), bf),
            pltpu.VMEM((chunks, 2, 4, rows, CHUNK), bf),
            pltpu.VMEM((chunks, 2, 2, 4, rows, CHUNK), bf),
            pltpu.VMEM((chunks, 2, rows, CHUNK), bf),
            pltpu.VMEM((chunks, 2, 2, rows, CHUNK), bf),
            pltpu.VMEM((chunks, rows, CHUNK), bf),
            dma((2,)),
            dma((2, micros, 2, PIECES)), dma((2, micros, 2, PIECES)),
            dma((micros, PIECES)), dma((micros, PIECES)),
            dma((micros, 2, 3)), dma((micros, 2, 3)),
            dma((micros, 2)), dma((micros, 2)),
            dma((micros, 4)), dma((micros, 4)),
            dma((micros, 4)), dma((micros, 4)),
            dma((2,)), dma((2,)),
            dma((micros,)), dma((micros,)),
            dma((micros, 2)), dma((micros, 2)),
            dma((chunks, 9)), dma((chunks, 9)),
        ],
        compiler_params=pltpu.CompilerParams(
            collective_id=1, has_side_effects=True, vmem_limit_bytes=60 * 1024 * 1024
        ),
        cost_estimate=pl.CostEstimate(
            flops=20 * 10**9, bytes_accessed=12 << 20, transcendentals=2 * 10**6
        ),
    )(scenes[:, 0], cotangent[:, 0], neighbours[:, 0], counts, w_in[0], w_out[0])
    return (outputs[None, :, None], grads[None, :, None], grad_in[None], grad_out[None])


def solution(mesh):
    in_specs = (
        P("dp", "view", None, None),
        P("dp", "view", None),
        P("dp", "view"),
        P("section", None, None),
        P("section", None, None),
        P("dp", "view", None, None),
    )
    out_specs = (
        P("section", "dp", "view", None, None),
        P("section", "dp", "view", None, None),
        P("section", ("view", "dp"), None),
        P("section", ("view", "dp"), None),
    )
    return jax.shard_map(
        on_device, mesh=mesh, in_specs=in_specs, out_specs=out_specs, check_vma=False
    )
```

```python
import functools
import math

import jax
import jax.numpy as jnp
from jax import lax
from jax.experimental import pallas as pl
from jax.experimental.pallas import tpu as pltpu
from jax.sharding import PartitionSpec as P

HEAD_DIM = 128
EPSILON = 1e-06
NEGATIVE = -1e30
MESH = pl.DeviceIdType.MESH
CHUNK = 512
PAIRS = ((6, 7), (0, 1), (2, 4), (3, 5))
FAR = tuple((dx, db) for dx in range(2) for db in range(4) if dx or db)
PIECES = 4
BLOCKS = 5
LAST = (((1,), (1,)), ((), ()))


def scene_kernel(
    scale, share,
    x_hbm, cot_hbm, nbr_ref, cnt_ref, win_hbm, wout_hbm,
    out_hbm, grad_hbm, gin_hbm, gout_hbm,
    out_ref, grad_ref, gin, gout, win, winT, wout, X, OG, N, QKV, AG, PR, IV, AT, FA, ST, SS, RD, NG,
    LN, LA, SN, SA, RP, RO, G, r1, r2, r3,
    wsem, osem, s_sp, r_sp, s_h, r_h, s_q, r_q, s_a, r_a, s_st, r_st, s_rd, r_rd,
    s_l, r_l, s_o, r_o, s_pj, r_pj, ss, rs, s_far, r_far,
):
    sec = lax.axis_index("section")
    view = lax.axis_index("view")
    zi = lax.axis_index("dp")
    core = lax.rem(view, 2)
    yi = lax.rem(view // 2, 4)
    xi = view // 8
    micros, toks, width = x_hbm.shape
    heads = width // HEAD_DIM
    relay = 3 - core
    scale_log2 = scale * math.log2(math.e)
    f32, bf = jnp.float32, jnp.bfloat16

    peer = {"view": view + 1 - 2 * core}
    ahead = {"view": lax.rem(view + 2, 16)}
    behind = {"view": lax.rem(view + 14, 16)}
    diag = {"view": lax.rem(view + 15 + 2 * core, 16)}
    other = {"section": 1 - sec}
    across = {"view": lax.rem(view + 8, 16)}

    def y_dev(step):
        return {"view": xi * 8 + lax.rem(yi + step + 4, 4) * 2 + core}

    def z_dev(step):
        return {"dp": lax.rem(zi + step + 4, 4)}

    loads = [
        pltpu.make_async_copy(win_hbm, win, wsem.at[0]),
        pltpu.make_async_copy(wout_hbm, wout, wsem.at[1]),
    ]
    own_in = [
        [pltpu.make_async_copy(x_hbm.at[m], X.at[m, 0], wsem.at[2 + m]) for m in range(micros)],
        [pltpu.make_async_copy(cot_hbm.at[m], OG.at[m, 0], wsem.at[2 + m]) for m in range(micros)],
    ]
    for s in range(2):
        @pl.when(sec == s)
        def _():
            for copy in own_in[s]:
                copy.start()

    for load in loads:
        load.start()

    partners = (
        peer, ahead, behind, diag, other, across, y_dev(1), y_dev(2), y_dev(3), z_dev(1),
        z_dev(2), z_dev(3),
    ) + tuple(
        dict(across, dp=lax.rem(zi + step, 4)) for step in range(1, 4)
    ) + tuple(
        {"view": (1 - xi) * 8 + lax.rem(yi + step, 4) * 2 + core} for step in range(1, 4)
    )
    barrier = pltpu.get_barrier_semaphore()
    for dev in partners:
        pl.semaphore_signal(barrier, inc=1, device_id=dev, device_id_type=MESH)
    pl.semaphore_wait(barrier, len(partners))

    def remote(src, dst, s, r, dev):
        return pltpu.make_async_remote_copy(
            src_ref=src, dst_ref=dst, send_sem=s, recv_sem=r, device_id=dev, device_id_type=MESH
        )

    def when_section(s):
        return pl.when(sec == s)

    step = toks // PIECES

    def spread(t, m, way, i):
        buf = (X, OG)[t]
        rows = pl.ds(i * step, step)
        return remote(
            buf.at[m, 0, rows], buf.at[m, 1 + way, rows],
            s_sp.at[t, m, way, i], r_sp.at[t, m, way, i], (ahead, behind)[way],
        )

    def hop(t, m, i):
        src, dst = ((out_ref, X), (grad_ref, OG))[t]
        rows = pl.ds(i * step, step)
        return remote(
            src.at[m, rows], dst.at[m, 0, rows], s_h.at[m, i], r_h.at[m, i], other
        )

    def share_qkv(m, which, j):
        src, dst = ((0, 1), (relay, 4))[which]
        cols = pl.ds(j * width, width)
        return remote(
            QKV.at[m, src, :, cols], QKV.at[m, dst, :, cols],
            s_q.at[m, which, j], r_q.at[m, which, j], peer,
        )

    def share_ag(m, which):
        src, dst = ((0, 1), (relay, 4))[which]
        return remote(AG.at[m, src], AG.at[m, dst], s_a.at[m, which], r_a.at[m, which], peer)

    ROUTES = {1: (1, peer), 3: (2, behind), 2: (3, ahead), 4: (4, diag)}

    def stats_to(m, block):
        target, dev = ROUTES[block]
        return remote(
            SS.at[m, target - 1], ST.at[m, block],
            s_st.at[m, block - 1], r_st.at[m, block - 1], dev,
        )

    def dots_to(m, block):
        return remote(
            RD.at[m, 0], RD.at[m, block],
            s_rd.at[m, block - 1], r_rd.at[m, block - 1], ROUTES[block][1],
        )

    own_toks = micros * toks

    def share_left(which):
        src, dst = ((SN, LN), (SA, LA))[which]
        return remote(
            src, dst.at[:, :, pl.ds(own_toks, own_toks)], s_l.at[which], r_l.at[which], peer
        )

    def share_og(m):
        return remote(RO.at[m], RO.at[micros + m], s_o.at[m], r_o.at[m], peer)

    def share_proj(m, which):
        half = width // 2
        cols = (
            pl.ds(0, width), pl.ds(width, half), pl.ds(2 * width, half),
            pl.ds(width + half, half), pl.ds(2 * width + half, half),
        )[which]
        return remote(
            RP.at[m, :, cols], RP.at[micros + m, :, cols],
            s_pj.at[m, which], r_pj.at[m, which], peer,
        )

    def start_spread(t, m):
        for i in range(PIECES):
            spread(t, m, 0, i).start()
            spread(t, m, 1, i).start()

    def wait_spread(t, m):
        for i in range(PIECES):
            spread(t, m, 0, i).wait_recv()
            spread(t, m, 1, i).wait_recv()

    def pass_piece(t, m, i):
        hop(t, m, i).wait_recv()
        spread(t, m, 0, i).start()
        spread(t, m, 1, i).start()

    def receive_hop(t, m):
        for i in range(PIECES):
            pass_piece(t, m, i)

    def store(which, m):
        src, dst = ((out_ref, out_hbm), (grad_ref, grad_hbm))[which]
        return pltpu.make_async_copy(src.at[m], dst.at[m], osem.at[which, m])

    def store_grads(which):
        src, dst = ((gin, gin_hbm), (gout, gout_hbm))[which]
        return pltpu.make_async_copy(src, dst, osem.at[2, which])

    side = 1 - 2 * core
    offsets = (0, side, -2, 2, -side)

    def live_block(m, k):
        if k == 0:
            return jnp.ones((1, toks), f32)
        live = jnp.float32(0.0)
        for j in range(nbr_ref.shape[1]):
            rel = lax.rem(nbr_ref[m, j] - view - offsets[k] + 32, 16)
            hit = jnp.logical_and(rel == 0, j < cnt_ref[m])
            live = jnp.where(hit, jnp.float32(1.0), live)
        return jnp.full((1, toks), live, f32)

    def norm_block(m, at):
        rows = X[m, at].astype(f32)
        factor = lax.rsqrt(jnp.mean(rows * rows, -1, keepdims=True) + EPSILON)
        normed = (rows * factor).astype(bf)
        N[at] = normed
        return factor, normed

    def keep_left(value, mine, theirs, m):
        parts = value.T.reshape(8, 2, width // 16, toks)
        cols = slice(m * toks, (m + 1) * toks)
        first, second = parts[:, 0], parts[:, 1]
        mine[:, :, cols] = jnp.where(core == 0, first, second)
        theirs[:, :, cols] = jnp.where(core == 0, second, first)

    def lanes():
        return lax.broadcasted_iota(jnp.int32, (toks, HEAD_DIM), 1)

    def project_own(m):
        factor, normed = norm_block(m, 0)
        FA[m] = factor
        for j in (1, 2, 0):
            cols = slice(j * width, (j + 1) * width)
            QKV[m, 0, :, cols] = jnp.dot(
                N[0], win[:, cols], preferred_element_type=f32
            ).astype(bf)
            share_qkv(m, 0, j).start()
        keep_left(normed, LN, SN, m)

    def forward(m):
        wait_spread(0, m)
        if m == 0:
            @when_section(0)
            def _():
                start_spread(0, 1)

        norm_block(m, 1)
        norm_block(m, 2)
        for block, shared in ((relay, True), (5 - relay, False)):
            for j in (1, 2):
                cols = slice(j * width, (j + 1) * width)
                QKV[m, block, :, cols] = jnp.dot(
                    N[block - 1], win[:, cols], preferred_element_type=f32
                ).astype(bf)
                if shared:
                    share_qkv(m, 1, j).start()
        near = jnp.dot(
            N[1:3].reshape(2 * toks, width), win[:, :width], preferred_element_type=f32
        ).astype(bf)
        QKV[m, 2:4, :, :width] = near.reshape(2, toks, width)
        share_qkv(m, 1, 0).start()
        for j in (1, 2):
            share_qkv(m, 0, j).wait_recv()
            share_qkv(m, 1, j).wait_recv()
        lives = [live_block(m, k) for k in range(BLOCKS)]
        live = jnp.concatenate(lives, 1) > 0.0
        stats = jnp.zeros((toks, HEAD_DIM), f32)
        for h in range(heads):
            cols = slice(h * HEAD_DIM, (h + 1) * HEAD_DIM)
            kcols = slice(width + h * HEAD_DIM, width + (h + 1) * HEAD_DIM)
            vcols = slice(2 * width + h * HEAD_DIM, 2 * width + (h + 1) * HEAD_DIM)
            scores = lax.dot_general(
                QKV[m, 0, :, cols], QKV[m, :, :, kcols].reshape(BLOCKS * toks, HEAD_DIM), LAST,
                preferred_element_type=f32,
            )
            masked = jnp.where(live, scores, NEGATIVE)
            top = jnp.max(masked, -1, keepdims=True)
            terms = jnp.exp2((masked - top) * scale_log2)
            inverse = 1.0 / jnp.sum(terms, -1, keepdims=True)
            low = terms.astype(bf)
            PR[m, h] = low
            IV[m, h] = inverse
            AT[m, :, cols] = (
                jnp.dot(
                    low, QKV[m, :, :, vcols].reshape(BLOCKS * toks, HEAD_DIM),
                    preferred_element_type=f32,
                ) * inverse
            ).astype(bf)
            stats = jnp.where(lanes() == h, top, stats)
            stats = jnp.where(lanes() == heads + h, inverse, stats)
            if m == 0 and h % 2 == 1:
                @when_section(1)
                def _():
                    pass_piece(0, 1, h // 2)
        if m == 0:
            @when_section(0)
            def _():
                loads[1].wait()

        branch = jnp.dot(AT[m], wout[...], preferred_element_type=f32)
        out_ref[m] = (X[m, 0].astype(f32) + branch).astype(bf)
        store(0, m).start()

        @when_section(0)
        def _():
            for i in range(PIECES):
                hop(0, m, i).start()

        turned = stats.T
        ST[m, 0] = turned[: 2 * heads]
        for k in range(1, BLOCKS):
            SS[m, k - 1, :heads] = jnp.where(lives[k] > 0.0, turned[:heads], -NEGATIVE)
            SS[m, k - 1, heads:] = turned[heads : 2 * heads]
        for block in ROUTES:
            stats_to(m, block).start()
        keep_left(AT[m], LA, SA, m)

    def own_ag(m):
        AG[m, 0] = lax.dot_general(
            OG[m, 0], wout[...], LAST, preferred_element_type=f32
        ).astype(bf)
        share_ag(m, 0).start()

    def near_ag(m):
        wait_spread(1, m)
        near = lax.dot_general(
            OG[m, 1:3].reshape(2 * toks, width), wout[...], LAST, preferred_element_type=f32
        ).astype(bf)
        AG[m, 2:4] = near.reshape(2, toks, width)
        share_ag(m, 1).start()

    def query_side(m):
        dots = jnp.zeros((toks, HEAD_DIM), f32)
        row_dots = []
        for h in range(heads):
            cols = slice(h * HEAD_DIM, (h + 1) * HEAD_DIM)
            row_dots.append(
                jnp.sum(
                    AG[m, 0, :, cols].astype(f32) * AT[m, :, cols].astype(f32), -1, keepdims=True
                )
            )
            dots = jnp.where(lanes() == h, row_dots[h], dots)
        RD[m, 0] = dots.T[:heads]
        for block in ROUTES:
            dots_to(m, block).start()
        RO[m] = OG[m, 0]
        share_og(m).start()
        for h in range(heads):
            cols = slice(h * HEAD_DIM, (h + 1) * HEAD_DIM)
            kcols = slice(width + h * HEAD_DIM, width + (h + 1) * HEAD_DIM)
            vcols = slice(2 * width + h * HEAD_DIM, 2 * width + (h + 1) * HEAD_DIM)
            terms = PR[m, h].astype(f32)
            prob_grad = lax.dot_general(
                AG[m, 0, :, cols], QKV[m, :, :, vcols].reshape(BLOCKS * toks, HEAD_DIM), LAST,
                preferred_element_type=f32,
            )
            score_grad = (terms * (prob_grad - row_dots[h])).astype(bf)
            RP[m, :, cols] = (
                jnp.dot(
                    score_grad, QKV[m, :, :, kcols].reshape(BLOCKS * toks, HEAD_DIM),
                    preferred_element_type=f32,
                ) * (IV[m, h] * scale)
            ).astype(bf)
        share_proj(m, 0).start()

    def backward(m):
        last = m == micros - 1

        @when_section(0)
        def _():
            receive_hop(1, m)
            own_ag(m)
            if m == 0:
                query_side(m)

        if m > 0:
            query_side(m)

        @when_section(0)
        def _():
            if last:
                open_pair(0)
            near_ag(m)
            if last:
                open_pair(1)
                stage(0, 1)

        for which in range(2):
            share_qkv(m, which, 0).wait_recv()
            share_ag(m, which).wait_recv()
        for block in ROUTES:
            stats_to(m, block).wait_recv()
            dots_to(m, block).wait_recv()

        def row(ref, h):
            return jnp.concatenate([ref[m, k, h : h + 1, :] for k in range(BLOCKS)], 1)

        for h in range(heads):
            cols = slice(h * HEAD_DIM, (h + 1) * HEAD_DIM)
            kcols = slice(width + h * HEAD_DIM, width + (h + 1) * HEAD_DIM)
            vcols = slice(2 * width + h * HEAD_DIM, 2 * width + (h + 1) * HEAD_DIM)
            queries = QKV[m, :, :, cols].reshape(BLOCKS * toks, HEAD_DIM)
            out_grads = AG[m, :, :, cols].reshape(BLOCKS * toks, HEAD_DIM)
            scores = lax.dot_general(
                QKV[m, 0, :, kcols], queries, LAST, preferred_element_type=f32
            )
            prob = jnp.exp2((scores - row(ST, h)) * scale_log2) * row(ST, heads + h)
            prob_grad = lax.dot_general(
                QKV[m, 0, :, vcols], out_grads, LAST, preferred_element_type=f32
            )
            score_grad = (prob * (prob_grad - row(RD, h))).astype(bf)
            RP[m, :, kcols] = (
                jnp.dot(score_grad, queries, preferred_element_type=f32) * scale
            ).astype(bf)
            RP[m, :, vcols] = jnp.dot(
                prob.astype(bf), out_grads, preferred_element_type=f32
            ).astype(bf)
            if h == heads // 2 - 1 or h == heads - 1:
                piece = 1 + 2 * (h // (heads // 2))
                share_proj(m, piece).start()
                share_proj(m, piece + 1).start()
            if last and h == heads // 2 - 1:
                @when_section(0)
                def _():
                    stage(1, 1)

    def finish(m):
        NG[...] = jnp.dot(RP[m], winT[...], preferred_element_type=f32)
        normed_grad = NG[...]
        factor = FA[m]
        unit = X[m, 0].astype(f32) * factor
        inner = jnp.mean(normed_grad * unit, -1, keepdims=True)
        grad_ref[m] = (
            OG[m, 0].astype(f32) + factor * (normed_grad - unit * inner)
        ).astype(bf)
        store(1, m).start()

    whole = slice(None)
    ring_at = (yi, zi)
    far_at = (zi, yi)

    def turn(value, by):
        return lax.rem(value + by, 4)

    def first(t, p, x_at, a):
        return G.at[t, p, x_at, a] if t == 0 else G.at[t, p, x_at, :, a]

    def second(t, p, x_at, b):
        a = ring_at[t]
        return G.at[t, p, x_at, a, b] if t == 0 else G.at[t, p, x_at, b, a]

    def far_dev(t, dx, db):
        x_to = xi if dx == 0 else 1 - xi
        if t == 0:
            return {"view": x_to * 8 + yi * 2 + core, "dp": turn(zi, db)}
        return {"view": x_to * 8 + turn(yi, db) * 2 + core}

    def ring(t, p, s):
        a = ring_at[t]
        dev = (y_dev, z_dev)[t]

        def make(k, src, dst, to):
            return remote(src, dst, ss.at[t, p, k], rs.at[t, p, k], to)

        if s == 0:
            return (
                make(0, first(t, p, 0, turn(a, 2)), r1.at[t, p, 0], dev(1)),
                make(1, first(t, p, 1, turn(a, 2)), r1.at[t, p, 1], dev(-1)),
            )
        return (
            make(2, first(t, p, whole, turn(a, 1)), r2.at[t, p, 0], dev(1)),
            make(3, first(t, p, whole, turn(a, 3)), r2.at[t, p, 1], dev(-1)),
        )

    def far(t, batch, k):
        dx, db = FAR[k]
        x_to = xi if dx == 0 else 1 - xi
        both = pl.ds(2 * batch, 2)
        return remote(
            second(t, both, x_to, turn(far_at[t], db)), r3.at[t, k, both],
            s_far.at[t, batch, k], r_far.at[t, batch, k], far_dev(t, dx, db),
        )

    def add_into(ref, *others):
        total = ref[...].astype(f32)
        for item in others:
            total = total + item[...].astype(f32)
        ref[...] = total.astype(bf)

    def stage(p, s):
        for t in range(2):
            n = PAIRS[p][t]
            a = ring_at[t]
            if s > 0:
                for copy in ring(t, p, s - 1):
                    copy.wait_recv()
            if s == 0:
                left = LA if n >= 6 else LN
                right, k = (RO, n - 6) if n >= 6 else (RP, n)
                part = jnp.dot(
                    left[...].reshape(left.shape[0] * left.shape[1], 2 * own_toks),
                    right[:, :, k * CHUNK : (k + 1) * CHUNK].reshape(2 * own_toks, CHUNK),
                    preferred_element_type=f32,
                )
                G[t, p] = part.astype(bf).reshape(G.shape[2:])
            elif s == 1:
                add_into(first(t, p, 0, turn(a, 1)), r1.at[t, p, 0])
                add_into(first(t, p, 1, turn(a, 3)), r1.at[t, p, 1])
            else:
                add_into(first(t, p, whole, a), r2.at[t, p, 0], r2.at[t, p, 1])
            if s < 2:
                for copy in ring(t, p, s):
                    copy.start()

    def send_far(batch):
        for t in range(2):
            for k in range(len(FAR)):
                far(t, batch, k).start()

    def take_far(batch):
        for t in range(2):
            for k in range(len(FAR)):
                far(t, batch, k).wait_recv()
            for p in (2 * batch, 2 * batch + 1):
                total = second(t, p, xi, far_at[t])[...].astype(f32)
                for k in range(len(FAR)):
                    total = total + r3[t, k, p].astype(f32)
                n = PAIRS[p][t]
                out, c = (gin, n) if n < 6 else (gout, n - 6)
                out[:, c * CHUNK : (c + 1) * CHUNK] = total * share

    def open_pair(p):
        if p == 0:
            for m in range(micros):
                share_og(m).wait_recv()
            share_left(1).wait_recv()
        elif p == 1:
            share_left(0).wait_recv()
            for m in range(micros):
                share_proj(m, 0).wait_recv()
        else:
            for m in range(micros):
                share_proj(m, 2 * p - 3).wait_recv()
                share_proj(m, 2 * p - 2).wait_recv()
        stage(p, 0)

    def turn_weights():
        @pl.loop(0, 3 * width // HEAD_DIM)
        def _(j):
            at = pl.ds(pl.multiple_of(j * HEAD_DIM, HEAD_DIM), HEAD_DIM)
            winT[at, :] = win[:, at].T

    @when_section(0)
    def _():
        for copy in own_in[0]:
            copy.wait()
        start_spread(0, 0)

    @when_section(1)
    def _():
        for m in range(micros):
            own_in[1][m].wait()
            start_spread(1, m)

    loads[0].wait()

    @when_section(1)
    def _():
        loads[1].wait()
        for m in range(micros):
            own_ag(m)
            near_ag(m)
        turn_weights()

    @when_section(1)
    def _():
        receive_hop(0, 0)

    project_own(0)

    @when_section(0)
    def _():
        project_own(1)

    forward(0)

    @when_section(1)
    def _():
        project_own(1)
        query_side(0)

    forward(1)

    @when_section(0)
    def _():
        turn_weights()

    for which in range(2):
        share_left(which).start()
    for m in range(micros):
        backward(m)
        if m < micros - 1:
            finish(m)

            @when_section(1)
            def _():
                for i in range(PIECES):
                    hop(1, m, i).start()

    @when_section(1)
    def _():
        finish(micros - 1)
        for i in range(PIECES):
            hop(1, micros - 1, i).start()
        open_pair(0)
        open_pair(1)
        stage(0, 1)
        stage(1, 1)

    open_pair(2)
    open_pair(3)

    @when_section(0)
    def _():
        finish(micros - 1)

    stage(2, 1)
    stage(3, 1)
    stage(0, 2)
    stage(1, 2)
    send_far(0)
    stage(2, 2)
    stage(3, 2)
    send_far(1)
    take_far(0)
    take_far(1)
    for which in range(2):
        store_grads(which).start()

    for which in range(2):
        for m in range(micros):
            store(which, m).wait()
        store_grads(which).wait()
    for m in range(micros):
        for t in range(2):
            for i in range(PIECES):
                spread(t, m, 0, i).wait_send()
                spread(t, m, 1, i).wait_send()
        for i in range(PIECES):
            @when_section(0)
            def _():
                hop(0, m, i).wait_send()

            @when_section(1)
            def _():
                hop(1, m, i).wait_send()
        for which in range(2):
            for j in range(3):
                share_qkv(m, which, j).wait_send()
            share_ag(m, which).wait_send()
        for which in range(5):
            share_proj(m, which).wait_send()
        for block in ROUTES:
            stats_to(m, block).wait_send()
            dots_to(m, block).wait_send()
        share_og(m).wait_send()
    for which in range(2):
        share_left(which).wait_send()
    for t in range(2):
        for p in range(len(PAIRS)):
            for s in range(2):
                for copy in ring(t, p, s):
                    copy.wait_send()
        for batch in range(2):
            for k in range(len(FAR)):
                far(t, batch, k).wait_send()


def hand_over_kernel(*refs):
    count = len(refs) // 2
    for i in range(count):
        refs[count + i][...] = refs[i][...]


def hand_over(*arrays):
    vm = pl.BlockSpec(memory_space=pltpu.VMEM)
    return pl.pallas_call(
        hand_over_kernel,
        out_shape=tuple(jax.ShapeDtypeStruct(a.shape, a.dtype) for a in arrays),
        in_specs=[vm] * len(arrays),
        out_specs=(vm,) * len(arrays),
    )(*arrays)


def on_device(scenes, neighbours, counts, w_in, w_out, cotangent):
    micros, _, toks, width = scenes.shape
    heads = width // HEAD_DIM
    share = 1.0 / (micros * lax.axis_size("dp"))
    pairs = len(PAIRS)
    rows = width // 64
    group = width // 16
    vm = pl.BlockSpec(memory_space=pltpu.VMEM)
    sm = pl.BlockSpec(memory_space=pltpu.SMEM)
    hbm = pl.BlockSpec(memory_space=pl.ANY)
    bf, f32 = jnp.bfloat16, jnp.float32
    sds = jax.ShapeDtypeStruct
    dma = pltpu.SemaphoreType.DMA
    outputs, grads, grad_in, grad_out = pl.pallas_call(
        functools.partial(scene_kernel, 1.0 / math.sqrt(HEAD_DIM), share),
        out_shape=(
            sds((micros, toks, width), bf),
            sds((micros, toks, width), bf),
            sds((rows, 3 * width), f32),
            sds((rows, width), f32),
        ),
        in_specs=[hbm, hbm, sm, sm, hbm, hbm],
        out_specs=(hbm,) * 4,
        scratch_shapes=[
            pltpu.VMEM((micros, toks, width), bf),
            pltpu.VMEM((micros, toks, width), bf),
            pltpu.VMEM((rows, 3 * width), f32),
            pltpu.VMEM((rows, width), f32),
            pltpu.VMEM((width, 3 * width), bf),
            pltpu.VMEM((3 * width, width), bf),
            pltpu.VMEM((width, width), bf),
            pltpu.VMEM((micros, 3, toks, width), bf),
            pltpu.VMEM((micros, 3, toks, width), bf),
            pltpu.VMEM((3, toks, width), bf),
            pltpu.VMEM((micros, BLOCKS, toks, 3 * width), bf),
            pltpu.VMEM((micros, BLOCKS, toks, width), bf),
            pltpu.VMEM((micros, heads, toks, BLOCKS * toks), bf),
            pltpu.VMEM((micros, heads, toks, 1), f32),
            pltpu.VMEM((micros, toks, width), bf),
            pltpu.VMEM((micros, toks, 1), f32),
            pltpu.VMEM((micros, BLOCKS, 2 * heads, toks), f32),
            pltpu.VMEM((micros, BLOCKS - 1, 2 * heads, toks), f32),
            pltpu.VMEM((micros, BLOCKS, heads, toks), f32),
            pltpu.VMEM((toks, width), f32),
            pltpu.VMEM((8, group, 2 * micros * toks), bf),
            pltpu.VMEM((8, group, 2 * micros * toks), bf),
            pltpu.VMEM((8, group, micros * toks), bf),
            pltpu.VMEM((8, group, micros * toks), bf),
            pltpu.VMEM((2 * micros, toks, 3 * width), bf),
            pltpu.VMEM((2 * micros, toks, width), bf),
            pltpu.VMEM((2, pairs, 2, 4, 4, rows, CHUNK), bf),
            pltpu.VMEM((2, pairs, 2, 4, rows, CHUNK), bf),
            pltpu.VMEM((2, pairs, 2, 2, 4, rows, CHUNK), bf),
            pltpu.VMEM((2, len(FAR), pairs, rows, CHUNK), bf),
            dma((2 + micros,)),
            dma((3, 2)),
            dma((2, micros, 2, PIECES)), dma((2, micros, 2, PIECES)),
            dma((micros, PIECES)), dma((micros, PIECES)),
            dma((micros, 2, 3)), dma((micros, 2, 3)),
            dma((micros, 2)), dma((micros, 2)),
            dma((micros, 4)), dma((micros, 4)),
            dma((micros, 4)), dma((micros, 4)),
            dma((2,)), dma((2,)),
            dma((micros,)), dma((micros,)),
            dma((micros, 5)), dma((micros, 5)),
            dma((2, pairs, 4)), dma((2, pairs, 4)),
            dma((2, 2, len(FAR))), dma((2, 2, len(FAR))),
        ],
        compiler_params=pltpu.CompilerParams(
            collective_id=1, has_side_effects=True, vmem_limit_bytes=62 * 1024 * 1024
        ),
        cost_estimate=pl.CostEstimate(
            flops=20 * 10**9, bytes_accessed=12 << 20, transcendentals=2 * 10**6
        ),
    )(scenes[:, 0], cotangent[:, 0], neighbours[:, 0], counts[:, 0], w_in[0], w_out[0])
    outputs, grads, grad_in, grad_out = hand_over(outputs, grads, grad_in, grad_out)
    return (outputs[None, :, None], grads[None, :, None], grad_in[None], grad_out[None])


def solution(mesh):
    in_specs = (
        P("dp", "view", None, None),
        P("dp", "view", None),
        P("dp", "view"),
        P("section", None, None),
        P("section", None, None),
        P("dp", "view", None, None),
    )
    out_specs = (
        P("section", "dp", "view", None, None),
        P("section", "dp", "view", None, None),
        P("section", ("view", "dp"), None),
        P("section", ("view", "dp"), None),
    )
    return jax.shard_map(
        on_device, mesh=mesh, in_specs=in_specs, out_specs=out_specs, check_vma=False
    )
```

```python
import functools
import math

import jax
import jax.numpy as jnp
from jax import lax
from jax.experimental import pallas as pl
from jax.experimental.pallas import tpu as pltpu
from jax.sharding import PartitionSpec as P

HEAD_DIM = 128
EPSILON = 1e-06
NEGATIVE = -1e30
MESH = pl.DeviceIdType.MESH
CHUNK = 512
PAIRS = ((6, 7), (0, 1), (2, 4), (3, 5))
FAR = tuple((dx, db) for dx in range(2) for db in range(4) if dx or db)
PIECES = 4
BLOCKS = 5
LAST = (((1,), (1,)), ((), ()))


def scene_kernel(
    scale, share,
    x_hbm, cot_hbm, nbr_ref, cnt_ref, win_hbm, wout_hbm,
    out_hbm, grad_hbm, gin_hbm, gout_hbm,
    out_ref, grad_ref, gin, gout, win, winT, wout, X, OG, N, QKV, AG, PR, IV, AT, FA, ST, SS, RD, NG,
    LN, LA, SN, SA, RP, RO, G, r1, r2, r3,
    wsem, osem, s_sp, r_sp, s_h, r_h, s_q, r_q, s_a, r_a, s_st, r_st, s_rd, r_rd,
    s_l, r_l, s_o, r_o, s_pj, r_pj, ss, rs, s_far, r_far,
):
    sec = lax.axis_index("section")
    view = lax.axis_index("view")
    zi = lax.axis_index("dp")
    core = lax.rem(view, 2)
    yi = lax.rem(view // 2, 4)
    xi = view // 8
    micros, toks, width = x_hbm.shape
    heads = width // HEAD_DIM
    relay = 3 - core
    scale_log2 = scale * math.log2(math.e)
    f32, bf = jnp.float32, jnp.bfloat16

    peer = {"view": view + 1 - 2 * core}
    ahead = {"view": lax.rem(view + 2, 16)}
    behind = {"view": lax.rem(view + 14, 16)}
    diag = {"view": lax.rem(view + 15 + 2 * core, 16)}
    other = {"section": 1 - sec}
    across = {"view": lax.rem(view + 8, 16)}

    def y_dev(step):
        return {"view": xi * 8 + lax.rem(yi + step + 4, 4) * 2 + core}

    def z_dev(step):
        return {"dp": lax.rem(zi + step + 4, 4)}

    loads = [
        pltpu.make_async_copy(win_hbm, win, wsem.at[0]),
        pltpu.make_async_copy(wout_hbm, wout, wsem.at[1]),
    ]
    own_in = [
        [pltpu.make_async_copy(x_hbm.at[m], X.at[m, 0], wsem.at[2 + m]) for m in range(micros)],
        [pltpu.make_async_copy(cot_hbm.at[m], OG.at[m, 0], wsem.at[2 + m]) for m in range(micros)],
    ]
    for s in range(2):
        @pl.when(sec == s)
        def _():
            for copy in own_in[s]:
                copy.start()

    for load in loads:
        load.start()

    partners = (
        peer, ahead, behind, diag, other, across, y_dev(1), y_dev(2), y_dev(3), z_dev(1),
        z_dev(2), z_dev(3),
    ) + tuple(
        dict(across, dp=lax.rem(zi + step, 4)) for step in range(1, 4)
    ) + tuple(
        {"view": (1 - xi) * 8 + lax.rem(yi + step, 4) * 2 + core} for step in range(1, 4)
    )
    barrier = pltpu.get_barrier_semaphore()
    for dev in partners:
        pl.semaphore_signal(barrier, inc=1, device_id=dev, device_id_type=MESH)
    pl.semaphore_wait(barrier, len(partners))

    def remote(src, dst, s, r, dev):
        return pltpu.make_async_remote_copy(
            src_ref=src, dst_ref=dst, send_sem=s, recv_sem=r, device_id=dev, device_id_type=MESH
        )

    def when_section(s):
        return pl.when(sec == s)

    step = toks // PIECES

    def spread(t, m, way, i):
        buf = (X, OG)[t]
        rows = pl.ds(i * step, step)
        return remote(
            buf.at[m, 0, rows], buf.at[m, 1 + way, rows],
            s_sp.at[t, m, way, i], r_sp.at[t, m, way, i], (ahead, behind)[way],
        )

    def hop(t, m, i):
        src, dst = ((out_ref, X), (grad_ref, OG))[t]
        rows = pl.ds(i * step, step)
        return remote(
            src.at[m, rows], dst.at[m, 0, rows], s_h.at[m, i], r_h.at[m, i], other
        )

    def share_qkv(m, which, j):
        src, dst = ((0, 1), (relay, 4))[which]
        cols = pl.ds(j * width, width)
        return remote(
            QKV.at[m, src, :, cols], QKV.at[m, dst, :, cols],
            s_q.at[m, which, j], r_q.at[m, which, j], peer,
        )

    def share_ag(m, which):
        src, dst = ((0, 1), (relay, 4))[which]
        return remote(AG.at[m, src], AG.at[m, dst], s_a.at[m, which], r_a.at[m, which], peer)

    ROUTES = {1: (1, peer), 3: (2, behind), 2: (3, ahead), 4: (4, diag)}

    def stats_to(m, block):
        target, dev = ROUTES[block]
        return remote(
            SS.at[m, target - 1], ST.at[m, block],
            s_st.at[m, block - 1], r_st.at[m, block - 1], dev,
        )

    def dots_to(m, block):
        return remote(
            RD.at[m, 0], RD.at[m, block],
            s_rd.at[m, block - 1], r_rd.at[m, block - 1], ROUTES[block][1],
        )

    own_toks = micros * toks

    def share_left(which):
        src, dst = ((SN, LN), (SA, LA))[which]
        return remote(
            src, dst.at[:, :, pl.ds(own_toks, own_toks)], s_l.at[which], r_l.at[which], peer
        )

    def share_og(m):
        return remote(RO.at[m], RO.at[micros + m], s_o.at[m], r_o.at[m], peer)

    def share_proj(m, which):
        half = width // 2
        cols = (
            pl.ds(0, width), pl.ds(width, half), pl.ds(2 * width, half),
            pl.ds(width + half, half), pl.ds(2 * width + half, half),
        )[which]
        return remote(
            RP.at[m, :, cols], RP.at[micros + m, :, cols],
            s_pj.at[m, which], r_pj.at[m, which], peer,
        )

    def start_spread(t, m):
        for i in range(PIECES):
            spread(t, m, 0, i).start()
            spread(t, m, 1, i).start()

    def wait_spread(t, m):
        for i in range(PIECES):
            spread(t, m, 0, i).wait_recv()
            spread(t, m, 1, i).wait_recv()

    def pass_piece(t, m, i):
        hop(t, m, i).wait_recv()
        spread(t, m, 0, i).start()
        spread(t, m, 1, i).start()

    def receive_hop(t, m):
        for i in range(PIECES):
            pass_piece(t, m, i)

    def store(which, m):
        src, dst = ((out_ref, out_hbm), (grad_ref, grad_hbm))[which]
        return pltpu.make_async_copy(src.at[m], dst.at[m], osem.at[which, m])

    def store_grads(which):
        src, dst = ((gin, gin_hbm), (gout, gout_hbm))[which]
        return pltpu.make_async_copy(src, dst, osem.at[2, which])

    side = 1 - 2 * core
    offsets = (0, side, -2, 2, -side)

    def live_block(m, k):
        if k == 0:
            return jnp.ones((1, toks), f32)
        live = jnp.float32(0.0)
        for j in range(nbr_ref.shape[1]):
            rel = lax.rem(nbr_ref[m, j] - view - offsets[k] + 32, 16)
            hit = jnp.logical_and(rel == 0, j < cnt_ref[m])
            live = jnp.where(hit, jnp.float32(1.0), live)
        return jnp.full((1, toks), live, f32)

    def norm_block(m, at):
        rows = X[m, at].astype(f32)
        factor = lax.rsqrt(jnp.mean(rows * rows, -1, keepdims=True) + EPSILON)
        normed = (rows * factor).astype(bf)
        N[at] = normed
        return factor, normed

    def keep_left(value, mine, theirs, m):
        parts = value.T.reshape(8, 2, width // 16, toks)
        cols = slice(m * toks, (m + 1) * toks)
        first, second = parts[:, 0], parts[:, 1]
        mine[:, :, cols] = jnp.where(core == 0, first, second)
        theirs[:, :, cols] = jnp.where(core == 0, second, first)

    def lanes():
        return lax.broadcasted_iota(jnp.int32, (toks, HEAD_DIM), 1)

    def project_own(m):
        factor, normed = norm_block(m, 0)
        FA[m] = factor
        for j in (1, 2, 0):
            cols = slice(j * width, (j + 1) * width)
            QKV[m, 0, :, cols] = jnp.dot(
                N[0], win[:, cols], preferred_element_type=f32
            ).astype(bf)
            share_qkv(m, 0, j).start()
        keep_left(normed, LN, SN, m)

    def forward(m):
        wait_spread(0, m)
        if m == 0:
            @when_section(0)
            def _():
                start_spread(0, 1)

        norm_block(m, 1)
        norm_block(m, 2)
        for block, shared in ((relay, True), (5 - relay, False)):
            for j in (1, 2):
                cols = slice(j * width, (j + 1) * width)
                QKV[m, block, :, cols] = jnp.dot(
                    N[block - 1], win[:, cols], preferred_element_type=f32
                ).astype(bf)
                if shared:
                    share_qkv(m, 1, j).start()
        near = jnp.dot(
            N[1:3].reshape(2 * toks, width), win[:, :width], preferred_element_type=f32
        ).astype(bf)
        QKV[m, 2:4, :, :width] = near.reshape(2, toks, width)
        share_qkv(m, 1, 0).start()
        for j in (1, 2):
            share_qkv(m, 0, j).wait_recv()
            share_qkv(m, 1, j).wait_recv()
        lives = [live_block(m, k) for k in range(BLOCKS)]
        live = jnp.concatenate(lives, 1) > 0.0
        stats = jnp.zeros((toks, HEAD_DIM), f32)
        for h in range(heads):
            cols = slice(h * HEAD_DIM, (h + 1) * HEAD_DIM)
            kcols = slice(width + h * HEAD_DIM, width + (h + 1) * HEAD_DIM)
            vcols = slice(2 * width + h * HEAD_DIM, 2 * width + (h + 1) * HEAD_DIM)
            scores = lax.dot_general(
                QKV[m, 0, :, cols], QKV[m, :, :, kcols].reshape(BLOCKS * toks, HEAD_DIM), LAST,
                preferred_element_type=f32,
            )
            masked = jnp.where(live, scores, NEGATIVE)
            top = jnp.max(masked, -1, keepdims=True)
            terms = jnp.exp2((masked - top) * scale_log2)
            inverse = 1.0 / jnp.sum(terms, -1, keepdims=True)
            low = terms.astype(bf)
            PR[m, h] = low
            IV[m, h] = inverse
            AT[m, :, cols] = (
                jnp.dot(
                    low, QKV[m, :, :, vcols].reshape(BLOCKS * toks, HEAD_DIM),
                    preferred_element_type=f32,
                ) * inverse
            ).astype(bf)
            stats = jnp.where(lanes() == h, top, stats)
            stats = jnp.where(lanes() == heads + h, inverse, stats)
            if m == 0 and h % 2 == 1:
                @when_section(1)
                def _():
                    pass_piece(0, 1, h // 2)
        if m == 0:
            @when_section(0)
            def _():
                loads[1].wait()

        branch = jnp.dot(AT[m], wout[...], preferred_element_type=f32)
        out_ref[m] = (X[m, 0].astype(f32) + branch).astype(bf)
        store(0, m).start()

        @when_section(0)
        def _():
            for i in range(PIECES):
                hop(0, m, i).start()

        turned = stats.T
        ST[m, 0] = turned[: 2 * heads]
        for k in range(1, BLOCKS):
            SS[m, k - 1, :heads] = jnp.where(lives[k] > 0.0, turned[:heads], -NEGATIVE)
            SS[m, k - 1, heads:] = turned[heads : 2 * heads]
        for block in ROUTES:
            stats_to(m, block).start()
        keep_left(AT[m], LA, SA, m)

    def own_ag(m):
        AG[m, 0] = lax.dot_general(
            OG[m, 0], wout[...], LAST, preferred_element_type=f32
        ).astype(bf)
        share_ag(m, 0).start()

    def near_ag(m):
        wait_spread(1, m)
        near = lax.dot_general(
            OG[m, 1:3].reshape(2 * toks, width), wout[...], LAST, preferred_element_type=f32
        ).astype(bf)
        AG[m, 2:4] = near.reshape(2, toks, width)
        share_ag(m, 1).start()

    def query_side(m):
        dots = jnp.zeros((toks, HEAD_DIM), f32)
        row_dots = []
        for h in range(heads):
            cols = slice(h * HEAD_DIM, (h + 1) * HEAD_DIM)
            row_dots.append(
                jnp.sum(
                    AG[m, 0, :, cols].astype(f32) * AT[m, :, cols].astype(f32), -1, keepdims=True
                )
            )
            dots = jnp.where(lanes() == h, row_dots[h], dots)
        RD[m, 0] = dots.T[:heads]
        for block in ROUTES:
            dots_to(m, block).start()
        RO[m] = OG[m, 0]
        share_og(m).start()
        for h in range(heads):
            cols = slice(h * HEAD_DIM, (h + 1) * HEAD_DIM)
            kcols = slice(width + h * HEAD_DIM, width + (h + 1) * HEAD_DIM)
            vcols = slice(2 * width + h * HEAD_DIM, 2 * width + (h + 1) * HEAD_DIM)
            terms = PR[m, h].astype(f32)
            prob_grad = lax.dot_general(
                AG[m, 0, :, cols], QKV[m, :, :, vcols].reshape(BLOCKS * toks, HEAD_DIM), LAST,
                preferred_element_type=f32,
            )
            score_grad = (terms * (prob_grad - row_dots[h])).astype(bf)
            RP[m, :, cols] = (
                jnp.dot(
                    score_grad, QKV[m, :, :, kcols].reshape(BLOCKS * toks, HEAD_DIM),
                    preferred_element_type=f32,
                ) * (IV[m, h] * scale)
            ).astype(bf)
        share_proj(m, 0).start()

    def key_side(m):
        last = m == micros - 1

        for which in range(2):
            share_qkv(m, which, 0).wait_recv()
            share_ag(m, which).wait_recv()
        for block in ROUTES:
            stats_to(m, block).wait_recv()
            dots_to(m, block).wait_recv()

        def row(ref, h):
            return jnp.concatenate([ref[m, k, h : h + 1, :] for k in range(BLOCKS)], 1)

        for h in range(heads):
            cols = slice(h * HEAD_DIM, (h + 1) * HEAD_DIM)
            kcols = slice(width + h * HEAD_DIM, width + (h + 1) * HEAD_DIM)
            vcols = slice(2 * width + h * HEAD_DIM, 2 * width + (h + 1) * HEAD_DIM)
            queries = QKV[m, :, :, cols].reshape(BLOCKS * toks, HEAD_DIM)
            out_grads = AG[m, :, :, cols].reshape(BLOCKS * toks, HEAD_DIM)
            scores = lax.dot_general(
                QKV[m, 0, :, kcols], queries, LAST, preferred_element_type=f32
            )
            prob = jnp.exp2((scores - row(ST, h)) * scale_log2) * row(ST, heads + h)
            prob_grad = lax.dot_general(
                QKV[m, 0, :, vcols], out_grads, LAST, preferred_element_type=f32
            )
            score_grad = (prob * (prob_grad - row(RD, h))).astype(bf)
            RP[m, :, kcols] = (
                jnp.dot(score_grad, queries, preferred_element_type=f32) * scale
            ).astype(bf)
            RP[m, :, vcols] = jnp.dot(
                prob.astype(bf), out_grads, preferred_element_type=f32
            ).astype(bf)
            if h == heads // 2 - 1 or h == heads - 1:
                piece = 1 + 2 * (h // (heads // 2))
                share_proj(m, piece).start()
                share_proj(m, piece + 1).start()
            if last and h == heads // 2 - 1:
                @when_section(0)
                def _():
                    stage(1, 1)

    def finish(m):
        NG[...] = jnp.dot(RP[m], winT[...], preferred_element_type=f32)
        normed_grad = NG[...]
        factor = FA[m]
        unit = X[m, 0].astype(f32) * factor
        inner = jnp.mean(normed_grad * unit, -1, keepdims=True)
        grad_ref[m] = (
            OG[m, 0].astype(f32) + factor * (normed_grad - unit * inner)
        ).astype(bf)
        store(1, m).start()

    whole = slice(None)
    ring_at = (yi, zi)
    far_at = (zi, yi)

    def turn(value, by):
        return lax.rem(value + by, 4)

    def first(t, p, x_at, a):
        return G.at[t, p, x_at, a] if t == 0 else G.at[t, p, x_at, :, a]

    def second(t, p, x_at, b):
        a = ring_at[t]
        return G.at[t, p, x_at, a, b] if t == 0 else G.at[t, p, x_at, b, a]

    def far_dev(t, dx, db):
        x_to = xi if dx == 0 else 1 - xi
        if t == 0:
            return {"view": x_to * 8 + yi * 2 + core, "dp": turn(zi, db)}
        return {"view": x_to * 8 + turn(yi, db) * 2 + core}

    def ring(t, p, s):
        a = ring_at[t]
        dev = (y_dev, z_dev)[t]

        def make(k, src, dst, to):
            return remote(src, dst, ss.at[t, p, k], rs.at[t, p, k], to)

        if s == 0:
            return (
                make(0, first(t, p, 0, turn(a, 2)), r1.at[t, p, 0], dev(1)),
                make(1, first(t, p, 1, turn(a, 2)), r1.at[t, p, 1], dev(-1)),
            )
        return (
            make(2, first(t, p, whole, turn(a, 1)), r2.at[t, p, 0], dev(1)),
            make(3, first(t, p, whole, turn(a, 3)), r2.at[t, p, 1], dev(-1)),
        )

    def far(t, batch, k):
        dx, db = FAR[k]
        x_to = xi if dx == 0 else 1 - xi
        both = pl.ds(2 * batch, 2)
        return remote(
            second(t, both, x_to, turn(far_at[t], db)), r3.at[t, k, both],
            s_far.at[t, batch, k], r_far.at[t, batch, k], far_dev(t, dx, db),
        )

    def add_into(ref, *others):
        total = ref[...].astype(f32)
        for item in others:
            total = total + item[...].astype(f32)
        ref[...] = total.astype(bf)

    def stage(p, s):
        for t in range(2):
            n = PAIRS[p][t]
            a = ring_at[t]
            if s > 0:
                for copy in ring(t, p, s - 1):
                    copy.wait_recv()
            if s == 0:
                left = LA if n >= 6 else LN
                right, k = (RO, n - 6) if n >= 6 else (RP, n)
                part = jnp.dot(
                    left[...].reshape(left.shape[0] * left.shape[1], 2 * own_toks),
                    right[:, :, k * CHUNK : (k + 1) * CHUNK].reshape(2 * own_toks, CHUNK),
                    preferred_element_type=f32,
                )
                G[t, p] = part.astype(bf).reshape(G.shape[2:])
            elif s == 1:
                add_into(first(t, p, 0, turn(a, 1)), r1.at[t, p, 0])
                add_into(first(t, p, 1, turn(a, 3)), r1.at[t, p, 1])
            else:
                add_into(first(t, p, whole, a), r2.at[t, p, 0], r2.at[t, p, 1])
            if s < 2:
                for copy in ring(t, p, s):
                    copy.start()

    def send_far(batch):
        for t in range(2):
            for k in range(len(FAR)):
                far(t, batch, k).start()

    def take_far(batch):
        for t in range(2):
            for k in range(len(FAR)):
                far(t, batch, k).wait_recv()
            for p in (2 * batch, 2 * batch + 1):
                total = second(t, p, xi, far_at[t])[...].astype(f32)
                for k in range(len(FAR)):
                    total = total + r3[t, k, p].astype(f32)
                n = PAIRS[p][t]
                out, c = (gin, n) if n < 6 else (gout, n - 6)
                out[:, c * CHUNK : (c + 1) * CHUNK] = total * share

    def open_pair(p):
        if p == 0:
            for m in range(micros):
                share_og(m).wait_recv()
            share_left(1).wait_recv()
        elif p == 1:
            share_left(0).wait_recv()
            for m in range(micros):
                share_proj(m, 0).wait_recv()
        else:
            for m in range(micros):
                share_proj(m, 2 * p - 3).wait_recv()
                share_proj(m, 2 * p - 2).wait_recv()
        stage(p, 0)

    def turn_weights():
        @pl.loop(0, 3 * width // HEAD_DIM)
        def _(j):
            at = pl.ds(pl.multiple_of(j * HEAD_DIM, HEAD_DIM), HEAD_DIM)
            winT[at, :] = win[:, at].T

    @when_section(0)
    def _():
        for copy in own_in[0]:
            copy.wait()
        start_spread(0, 0)

    @when_section(1)
    def _():
        for m in range(micros):
            own_in[1][m].wait()
            start_spread(1, m)

    loads[0].wait()

    @when_section(1)
    def _():
        loads[1].wait()
        for m in range(micros):
            own_ag(m)
            near_ag(m)
        turn_weights()

    @when_section(1)
    def _():
        receive_hop(0, 0)

    project_own(0)

    @when_section(0)
    def _():
        project_own(1)

    forward(0)

    @when_section(1)
    def _():
        project_own(1)
        query_side(0)
        key_side(0)
        finish(0)
        for i in range(PIECES):
            hop(1, 0, i).start()

    forward(1)

    for which in range(2):
        share_left(which).start()
    @when_section(0)
    def _():
        turn_weights()
        receive_hop(1, 0)
        own_ag(0)
        query_side(0)
        near_ag(0)
        key_side(0)
        finish(0)
        receive_hop(1, 1)
        own_ag(1)

    query_side(1)

    @when_section(0)
    def _():
        open_pair(0)
        near_ag(1)
        open_pair(1)
        stage(0, 1)

    key_side(1)

    @when_section(1)
    def _():
        finish(micros - 1)
        for i in range(PIECES):
            hop(1, micros - 1, i).start()
        open_pair(0)
        open_pair(1)
        stage(0, 1)
        stage(1, 1)

    open_pair(2)
    open_pair(3)

    @when_section(0)
    def _():
        finish(micros - 1)

    stage(2, 1)
    stage(3, 1)
    stage(0, 2)
    stage(1, 2)
    send_far(0)
    stage(2, 2)
    stage(3, 2)
    send_far(1)
    take_far(0)
    take_far(1)
    for which in range(2):
        store_grads(which).start()

    for which in range(2):
        for m in range(micros):
            store(which, m).wait()
        store_grads(which).wait()
    for m in range(micros):
        for t in range(2):
            for i in range(PIECES):
                spread(t, m, 0, i).wait_send()
                spread(t, m, 1, i).wait_send()
        for i in range(PIECES):
            @when_section(0)
            def _():
                hop(0, m, i).wait_send()

            @when_section(1)
            def _():
                hop(1, m, i).wait_send()
        for which in range(2):
            for j in range(3):
                share_qkv(m, which, j).wait_send()
            share_ag(m, which).wait_send()
        for which in range(5):
            share_proj(m, which).wait_send()
        for block in ROUTES:
            stats_to(m, block).wait_send()
            dots_to(m, block).wait_send()
        share_og(m).wait_send()
    for which in range(2):
        share_left(which).wait_send()
    for t in range(2):
        for p in range(len(PAIRS)):
            for s in range(2):
                for copy in ring(t, p, s):
                    copy.wait_send()
        for batch in range(2):
            for k in range(len(FAR)):
                far(t, batch, k).wait_send()


def hand_over_kernel(*refs):
    count = len(refs) // 2
    for i in range(count):
        refs[count + i][...] = refs[i][...]


def hand_over(*arrays):
    vm = pl.BlockSpec(memory_space=pltpu.VMEM)
    return pl.pallas_call(
        hand_over_kernel,
        out_shape=tuple(jax.ShapeDtypeStruct(a.shape, a.dtype) for a in arrays),
        in_specs=[vm] * len(arrays),
        out_specs=(vm,) * len(arrays),
    )(*arrays)


def on_device(scenes, neighbours, counts, w_in, w_out, cotangent):
    micros, _, toks, width = scenes.shape
    heads = width // HEAD_DIM
    share = 1.0 / (micros * lax.axis_size("dp"))
    pairs = len(PAIRS)
    rows = width // 64
    group = width // 16
    vm = pl.BlockSpec(memory_space=pltpu.VMEM)
    sm = pl.BlockSpec(memory_space=pltpu.SMEM)
    hbm = pl.BlockSpec(memory_space=pl.ANY)
    bf, f32 = jnp.bfloat16, jnp.float32
    sds = jax.ShapeDtypeStruct
    dma = pltpu.SemaphoreType.DMA
    outputs, grads, grad_in, grad_out = pl.pallas_call(
        functools.partial(scene_kernel, 1.0 / math.sqrt(HEAD_DIM), share),
        out_shape=(
            sds((micros, toks, width), bf),
            sds((micros, toks, width), bf),
            sds((rows, 3 * width), f32),
            sds((rows, width), f32),
        ),
        in_specs=[hbm, hbm, sm, sm, hbm, hbm],
        out_specs=(hbm,) * 4,
        scratch_shapes=[
            pltpu.VMEM((micros, toks, width), bf),
            pltpu.VMEM((micros, toks, width), bf),
            pltpu.VMEM((rows, 3 * width), f32),
            pltpu.VMEM((rows, width), f32),
            pltpu.VMEM((width, 3 * width), bf),
            pltpu.VMEM((3 * width, width), bf),
            pltpu.VMEM((width, width), bf),
            pltpu.VMEM((micros, 3, toks, width), bf),
            pltpu.VMEM((micros, 3, toks, width), bf),
            pltpu.VMEM((3, toks, width), bf),
            pltpu.VMEM((micros, BLOCKS, toks, 3 * width), bf),
            pltpu.VMEM((micros, BLOCKS, toks, width), bf),
            pltpu.VMEM((micros, heads, toks, BLOCKS * toks), bf),
            pltpu.VMEM((micros, heads, toks, 1), f32),
            pltpu.VMEM((micros, toks, width), bf),
            pltpu.VMEM((micros, toks, 1), f32),
            pltpu.VMEM((micros, BLOCKS, 2 * heads, toks), f32),
            pltpu.VMEM((micros, BLOCKS - 1, 2 * heads, toks), f32),
            pltpu.VMEM((micros, BLOCKS, heads, toks), f32),
            pltpu.VMEM((toks, width), f32),
            pltpu.VMEM((8, group, 2 * micros * toks), bf),
            pltpu.VMEM((8, group, 2 * micros * toks), bf),
            pltpu.VMEM((8, group, micros * toks), bf),
            pltpu.VMEM((8, group, micros * toks), bf),
            pltpu.VMEM((2 * micros, toks, 3 * width), bf),
            pltpu.VMEM((2 * micros, toks, width), bf),
            pltpu.VMEM((2, pairs, 2, 4, 4, rows, CHUNK), bf),
            pltpu.VMEM((2, pairs, 2, 4, rows, CHUNK), bf),
            pltpu.VMEM((2, pairs, 2, 2, 4, rows, CHUNK), bf),
            pltpu.VMEM((2, len(FAR), pairs, rows, CHUNK), bf),
            dma((2 + micros,)),
            dma((3, 2)),
            dma((2, micros, 2, PIECES)), dma((2, micros, 2, PIECES)),
            dma((micros, PIECES)), dma((micros, PIECES)),
            dma((micros, 2, 3)), dma((micros, 2, 3)),
            dma((micros, 2)), dma((micros, 2)),
            dma((micros, 4)), dma((micros, 4)),
            dma((micros, 4)), dma((micros, 4)),
            dma((2,)), dma((2,)),
            dma((micros,)), dma((micros,)),
            dma((micros, 5)), dma((micros, 5)),
            dma((2, pairs, 4)), dma((2, pairs, 4)),
            dma((2, 2, len(FAR))), dma((2, 2, len(FAR))),
        ],
        compiler_params=pltpu.CompilerParams(
            collective_id=1, has_side_effects=True, vmem_limit_bytes=62 * 1024 * 1024
        ),
        cost_estimate=pl.CostEstimate(
            flops=20 * 10**9, bytes_accessed=12 << 20, transcendentals=2 * 10**6
        ),
    )(scenes[:, 0], cotangent[:, 0], neighbours[:, 0], counts[:, 0], w_in[0], w_out[0])
    outputs, grads, grad_in, grad_out = hand_over(outputs, grads, grad_in, grad_out)
    return (outputs[None, :, None], grads[None, :, None], grad_in[None], grad_out[None])


def solution(mesh):
    in_specs = (
        P("dp", "view", None, None),
        P("dp", "view", None),
        P("dp", "view"),
        P("section", None, None),
        P("section", None, None),
        P("dp", "view", None, None),
    )
    out_specs = (
        P("section", "dp", "view", None, None),
        P("section", "dp", "view", None, None),
        P("section", ("view", "dp"), None),
        P("section", ("view", "dp"), None),
    )
    return jax.shard_map(
        on_device, mesh=mesh, in_specs=in_specs, out_specs=out_specs, check_vma=False
    )
```
